32 devices in a mesh: section: 4 (over z), chan: 8 (over y, x, core).
Axes of the slice: x: 2, y: 2, z: 4, core: 2. Of those that a mesh axis runs over, the one named last changes fastest.
Arguments:
- inputs: bfloat16 [4, 256, 4096], P(None, None, 'chan'), may hold values from -6 to 6
- labels: int32 [4, 256], replicated, may hold values from 0 to 2
- conv_weight: bfloat16 [4, 9, 64, 4096], P('section', None, None, 'chan'), may hold values from -0.25 to 0.25
- point_weight: bfloat16 [4, 4096, 4096], P('section', 'chan'), may hold values from -0.125 to 0.125
- head_weight: bfloat16 [4096, 3], P('chan'), may hold values from -0.09375 to 0.09375
Outputs:
- grad_point: float32 [4, 4096, 4096], P('section', 'chan')
- grad_conv: float32 [4, 9, 64, 4096], P('section', None, None, 'chan')
The draws below stay inside these ranges and needn't reach their ends.
All inputs are finite; a program needn't handle non-finite values.
Results may differ from the reference program's by a relative error of at most 0.035.
Values may be sent and summed in bfloat16 or wider, within the bound.
No kernel may reach another device: no remote copies, remote signals or barrier semaphores. Data moves between devices by JAX's collectives and lax.ppermute only.
A program may use at most 192 MiB of HBM per device.

```python
import jax
import jax.numpy as jnp
from jax import lax

C = 4096
GW = 64
TAPS = 9
BLOCKS = 4
MICRO = 4
T_MB = 256
CLASSES = 3
LOSS_SCALE = 2048
N_CHAN = 8


def plant(drawn, rng, smallest, high):
    place = [jax.random.randint(jax.random.fold_in(rng, axis), (), 0, length) for axis, length in enumerate(drawn.shape)]
    widest = drawn.shape.index(max(drawn.shape))
    neighbour = place[:widest] + [(place[widest] + 1) % drawn.shape[widest]] + place[widest + 1:]
    return drawn.at[tuple(place)].set(smallest).at[tuple(neighbour)].set(high)


def spiked(entries, rng, source, target, parts, factor):
    owner, partner = [(jnp.arange(entries.shape[position]) // (entries.shape[position] // parts)).reshape([-1 if axis == position else 1 for axis in range(entries.ndim)]) for position in (source, target)]
    chosen = jax.random.permutation(rng, parts)[partner]
    strong = (owner == chosen) | (owner == (partner + parts // 2) % parts)
    return jnp.where(strong, factor * entries, entries)


def levels(stream_key, dims, cuts, least, high):
    def one(dim, shards_of):
        steps = jax.random.uniform(jax.random.fold_in(jax.random.fold_in(stream_key, 6), dim), (shards_of,), jnp.float32, least / len(cuts), high / len(cuts))
        return jnp.repeat(jnp.exp(steps), dims[dim] // shards_of).reshape((-1,) + (1,) * (len(dims) - dim - 1))

    factor_of = one(*cuts[0])
    for cut in cuts[1:]:
        factor_of = factor_of * one(*cut)
    return factor_of


def scatter_about(stream_key, extent, deviation, most, shards=(), dtype=jnp.bfloat16):
    loudness = levels(stream_key, extent, shards, -0.22, 0.18) if shards else 1.0
    values = jax.random.normal(stream_key, extent, jnp.float32) * deviation * loudness
    return jnp.minimum(jnp.maximum(values, -most), most).astype(dtype)


def heavy_noise(stream_key, shape, spread, bound, split, heavy, held_as=jnp.bfloat16):
    drawn = spread * jax.random.normal(stream_key, shape, jnp.float32)
    if split:
        drawn = drawn * levels(stream_key, shape, split, -0.22, 0.18)
    return jnp.clip(spiked(drawn, jax.random.fold_in(stream_key, 3), *heavy), -bound, bound).astype(held_as)


def setup_inputs(seed: int = 0) -> dict:
    key_of = jax.random.split(jax.random.key(seed), 6)
    return {
        "inputs": scatter_about(key_of[0], (MICRO, T_MB, C), 1.0, 6.0, ((2, 8),)),
        "labels": plant(jax.random.randint(key_of[1], (MICRO, T_MB), 0, CLASSES), jax.random.fold_in(key_of[1], 1), 0, CLASSES - 1).astype(jnp.int32),
        "conv_weight": scatter_about(key_of[2], (BLOCKS, TAPS, GW, C), (TAPS * GW) ** -0.5, 0.25, ((0, 4), (3, 8))),
        "point_weight": heavy_noise(key_of[3], (BLOCKS, C, C), C ** -0.5, 0.125, ((0, 4), (1, 8)), (1, 2, 8, 2.0)),
        "head_weight": scatter_about(key_of[4], (C, CLASSES), C ** -0.5, 0.09375, ((0, 8),)),
    }


def conv_apply(field, kernel, groups):
    half = TAPS // 2
    return lax.conv_general_dilated(field[None], kernel, (1,), [(half, half)], dimension_numbers=('NWC', 'WIO', 'NWC'), feature_group_count=groups, precision=lax.Precision.HIGHEST)[0]

def turn_kernel(kernel):
    taps, width, chans = kernel.shape
    shaped = kernel.reshape(taps, width, chans // width, width)
    shaped = jnp.transpose(shaped, (0, 3, 2, 1))[::-1]
    return shaped.reshape(taps, width, chans)

def kernel_grad(field, grads, width):
    half = TAPS // 2
    steps, chans = field.shape
    padded = jnp.pad(field, ((half, half), (0, 0)))
    grads3 = grads.reshape(steps, chans // width, width)
    pieces = []
    for k in range(TAPS):
        shifted = padded[k:k + steps].reshape(steps, chans // width, width)
        pieces.append(jnp.einsum('tgi,tgo->igo', shifted, grads3).reshape(width, chans))
    return jnp.stack(pieces)

def pointwise(act, weight):
    rows = C // N_CHAN
    total = jnp.zeros((act.shape[0], C), jnp.float32)
    for j in range(N_CHAN):
        part = jnp.dot(act[:, j * rows:(j + 1) * rows], weight[j * rows:(j + 1) * rows], preferred_element_type=jnp.float32)
        rounded = lax.optimization_barrier(part.astype(jnp.bfloat16))
        total = total + rounded.astype(jnp.float32)
    return total

def reference(inputs, labels, conv_weight, point_weight, head_weight):
    groups = C // GW
    grad_point = [jnp.zeros((C, C), jnp.float32) for b in range(BLOCKS)]
    grad_conv = [jnp.zeros((TAPS, GW, C), jnp.float32) for b in range(BLOCKS)]
    head32 = head_weight.astype(jnp.float32)
    for m in range(MICRO):
        state = inputs[m]
        saved = []
        for b in range(BLOCKS):
            saved.append(state)
            conv_out = conv_apply(state.astype(jnp.float32), conv_weight[b].astype(jnp.float32), groups)
            act = (conv_out * jax.nn.sigmoid(conv_out)).astype(jnp.bfloat16)
            mixed = pointwise(act, point_weight[b])
            state = (state.astype(jnp.float32) + mixed).astype(jnp.bfloat16)
        scores = jnp.dot(state, head_weight, preferred_element_type=jnp.float32)
        onehot = (labels[m][:, None] == jnp.arange(CLASSES)[None, :]).astype(jnp.float32)
        top = (jax.nn.sigmoid(scores) - onehot) * (LOSS_SCALE / (MICRO * T_MB))
        back = jnp.dot(top, head32.T, precision=lax.Precision.HIGHEST).astype(jnp.bfloat16)
        for b in range(BLOCKS - 1, -1, -1):
            state_b = saved[b]
            conv_out = conv_apply(state_b.astype(jnp.float32), conv_weight[b].astype(jnp.float32), groups)
            sig = jax.nn.sigmoid(conv_out)
            act = (conv_out * sig).astype(jnp.bfloat16)
            act_grad = lax.dot_general(back, point_weight[b], (((1,), (1,)), ((), ())), preferred_element_type=jnp.float32)
            conv_grad = (act_grad * sig * (1.0 + conv_out * (1.0 - sig))).astype(jnp.bfloat16)
            grad_point[b] = grad_point[b] + lax.dot_general(act, back, (((0,), (0,)), ((), ())), preferred_element_type=jnp.float32)
            grad_conv[b] = grad_conv[b] + kernel_grad(state_b.astype(jnp.float32), conv_grad.astype(jnp.float32), GW)
            input_grad = conv_apply(conv_grad.astype(jnp.float32), turn_kernel(conv_weight[b].astype(jnp.float32)), groups)
            back = (back.astype(jnp.float32) + input_grad).astype(jnp.bfloat16)
    return (jnp.stack(grad_point), jnp.stack(grad_conv))
```

```python
import jax
import jax.numpy as jnp
from jax import lax
from jax.experimental import pallas as pl
from jax.experimental.pallas import tpu as pltpu
from jax.sharding import PartitionSpec as P

CLASSES = 3
LOSS_SCALE = 2048
CROWS = 8
PAD = 8
F32 = jnp.float32
BF16 = jnp.bfloat16
NT = (((1,), (1,)), ((), ()))
TN = (((0,), (0,)), ((), ()))


def params(mib):
    return pltpu.CompilerParams(vmem_limit_bytes=mib * 1024 * 1024)


def cost(flops, moved):
    return pl.CostEstimate(flops=int(flops), bytes_accessed=int(moved), transcendentals=0)


def vmem_spec():
    return pl.BlockSpec(memory_space=pltpu.VMEM)


def smem_spec():
    return pl.BlockSpec(memory_space=pltpu.SMEM)


def block_diagonal(kernel, pack):
    taps, width, chans = kernel.shape
    shaped = jnp.transpose(kernel.reshape(taps, width, chans // pack, pack), (0, 2, 1, 3))
    tiled = jnp.tile(shaped, (1, 1, pack // width, 1))
    row = jnp.arange(pack)[:, None] // width
    col = jnp.arange(pack)[None, :] // width
    return jnp.where(row == col, tiled, jnp.zeros_like(tiled))


def fill_padded(padded, field):
    steps, chans = field.shape
    padded[0:PAD, :] = jnp.zeros((PAD, chans), F32)
    padded[PAD : PAD + steps, :] = field
    padded[PAD + steps : PAD + steps + PAD, :] = jnp.zeros((PAD, chans), F32)


def conv_kernel(first, sel_ref, fresh_ref, recv_ref, wd_ref, *refs):
    if first:
        state_ref, act_ref, deriv_ref, act_all, state_all, padded = refs
    else:
        unused_a, unused_s, state_ref, act_ref, deriv_ref, act_all, state_all, padded = refs
    taps, packs, pack, unused = wd_ref.shape
    steps, chans = fresh_ref.shape
    half = taps // 2
    state = jnp.where(sel_ref[1] == 0, fresh_ref[...], recv_ref[...])
    state_ref[...] = state
    state_all[0] = state
    fill_padded(padded, state.astype(F32))
    for p in range(packs):
        cols = slice(p * pack, (p + 1) * pack)
        out = jnp.zeros((steps, pack), F32)
        for k in range(taps):
            start = PAD + k - half
            out = out + jnp.dot(
                padded[start : start + steps, cols].astype(BF16), wd_ref[k, p], preferred_element_type=F32
            )
        sig = jax.nn.sigmoid(out)
        act = (out * sig).astype(BF16)
        act_ref[:, cols] = act
        act_all[0, :, cols] = act
        deriv_ref[:, cols] = sig * (1.0 + out * (1.0 - sig))


def conv_forward(sel, fresh, recv, wd, micro, act_all, state_all):
    steps, chans = fresh.shape
    first = act_all is None
    slot = lambda i, sel: (sel[0], 0, 0)
    whole = lambda shape: pl.BlockSpec(shape, lambda i, sel: (0,) * len(shape))
    args = (sel, fresh, recv, wd) + (() if first else (act_all, state_all))
    any_spec = pl.BlockSpec(memory_space=pl.ANY)
    full = jax.ShapeDtypeStruct((micro + 1, steps, chans), BF16)
    one = jax.ShapeDtypeStruct((steps, chans), BF16)
    return pl.pallas_call(
        lambda *refs: conv_kernel(first, *refs),
        grid_spec=pltpu.PrefetchScalarGridSpec(
            num_scalar_prefetch=1,
            grid=(1,),
            in_specs=[whole((steps, chans)), whole((steps, chans)), whole(wd.shape)] + ([] if first else [any_spec] * 2),
            out_specs=[whole((steps, chans))] * 3
            + [pl.BlockSpec((1, steps, chans), slot), pl.BlockSpec((1, steps, chans), slot)],
            scratch_shapes=[pltpu.VMEM((steps + 2 * PAD, chans), F32)],
        ),
        out_shape=[one, one, jax.ShapeDtypeStruct((steps, chans), F32), full, full],
        input_output_aliases={} if first else {4: 3, 5: 4},
        compiler_params=params(32),
        cost_estimate=cost(2 * steps * chans * wd.shape[2] * wd.shape[0], 2 * wd.size),
        name="conv_forward",
    )(*args)


def mix_kernel(a_ref, b_ref, wa_ref, wb_ref, out_ref):
    total = jnp.dot(a_ref[...], wa_ref[...], preferred_element_type=F32)
    total = total + jnp.dot(b_ref[...], wb_ref[...], preferred_element_type=F32)
    out_ref[...] = total.astype(out_ref.dtype)


def mix_add_kernel(a_ref, b_ref, wa_ref, wb_ref, state_ref, out_ref):
    total = jnp.dot(a_ref[...], wa_ref[...], preferred_element_type=F32)
    total = total + jnp.dot(b_ref[...], wb_ref[...], preferred_element_type=F32)
    out_ref[...] = total + state_ref[...].astype(F32)


def mix(act, act_twin, wa, wb, state=None):
    steps, chans = act.shape
    args = (act, act_twin, wa, wb) + (() if state is None else (state,))
    return pl.pallas_call(
        mix_kernel if state is None else mix_add_kernel,
        in_specs=[vmem_spec()] * len(args),
        out_specs=vmem_spec(),
        out_shape=jax.ShapeDtypeStruct((steps, wa.shape[1]), BF16 if state is None else F32),
        compiler_params=params(16),
        cost_estimate=cost(4 * steps * chans * wa.shape[1], 4 * wa.size),
        name="mix",
    )(*args)


def sum_kernel(with_head, own_ref, *refs):
    if with_head:
        *parts, head_ref, out_ref, score_ref = refs
    else:
        *parts, out_ref = refs
    total = own_ref[...]
    for part in parts:
        total = total + part[...].astype(F32)
    state = total.astype(BF16)
    out_ref[...] = state
    if with_head:
        score_ref[...] = lax.dot_general(head_ref[...], state, NT, preferred_element_type=F32)


def sum_state(own, parts, head_rows=None):
    steps, chans = own.shape
    args = (own, *parts) + (() if head_rows is None else (head_rows,))
    shapes = [jax.ShapeDtypeStruct((steps, chans), BF16)]
    if head_rows is not None:
        shapes.append(jax.ShapeDtypeStruct((CROWS, steps), F32))
    return pl.pallas_call(
        lambda *refs: sum_kernel(head_rows is not None, *refs),
        in_specs=[vmem_spec()] * len(args),
        out_specs=[vmem_spec()] * len(shapes),
        out_shape=shapes,
        compiler_params=params(16),
        cost_estimate=cost(steps * chans * 8, 8 * steps * chans),
        name="sum_state",
    )(*args)


def top_kernel(scale, sel_ref, score_ref, label_ref, head_ref, recv_ref, out_ref):
    @pl.when(sel_ref[2] == 1)
    def _():
        score = score_ref[...]
        row = lax.broadcasted_iota(jnp.int32, score.shape, 0)
        hot = (label_ref[...] == row).astype(F32)
        top = (jax.nn.sigmoid(score) - hot) * scale
        top = jnp.where(row < CLASSES, top, 0.0)
        out_ref[...] = lax.dot_general(
            top, head_ref[...].astype(F32), TN, preferred_element_type=F32, precision=lax.Precision.HIGHEST
        ).astype(BF16)

    @pl.when(sel_ref[2] == 0)
    def _():
        out_ref[...] = recv_ref[...]


def top_back(sel, score, label_row, head_rows, recv, scale):
    return pl.pallas_call(
        lambda *refs: top_kernel(scale, *refs),
        in_specs=[smem_spec()] + [vmem_spec()] * 4,
        out_specs=vmem_spec(),
        out_shape=jax.ShapeDtypeStruct(recv.shape, BF16),
        compiler_params=params(16),
        name="top_back",
    )(sel, score, label_row, head_rows, recv)


def fold_kernel(has_acc, pairs, *refs):
    out_ref = refs[-1]
    offset = 1 if has_acc else 0
    total = refs[0][...] if has_acc else None
    for i in range(pairs):
        part = lax.dot_general(
            refs[offset + 2 * i][...], refs[offset + 2 * i + 1][...], NT, preferred_element_type=F32
        )
        total = part if total is None else total + part
    out_ref[...] = total


def fold(acc, pairs):
    args = (() if acc is None else (acc,)) + tuple(x for pair in pairs for x in pair)
    piece, weights = pairs[0]
    return pl.pallas_call(
        lambda *refs: fold_kernel(acc is not None, len(pairs), *refs),
        in_specs=[vmem_spec()] * len(args),
        out_specs=vmem_spec(),
        out_shape=jax.ShapeDtypeStruct((piece.shape[0], weights.shape[0]), F32),
        compiler_params=params(24),
        cost_estimate=cost(2 * piece.size * weights.shape[0] * len(pairs), 2 * weights.size * len(pairs)),
        name="fold",
    )(*args)


def back_kernel(first, pieces, sel_ref, acc_ref, deriv_ref, wd_ref, *refs):
    piece_refs = refs[:pieces]
    rest = refs[pieces:]
    if not first:
        rest = rest[2:]
    out_ref, back_all, grad_all, padded = rest
    taps, packs, pack, unused = wd_ref.shape
    steps, chans = acc_ref.shape
    half = taps // 2
    for i in range(pieces):
        back_all[0, i] = piece_refs[i][...]
    grad = (acc_ref[...] * deriv_ref[...]).astype(BF16)
    grad_all[0] = grad
    fill_padded(padded, grad.astype(F32))
    for p in range(packs):
        cols = slice(p * pack, (p + 1) * pack)
        out = piece_refs[0][:, cols].astype(F32)
        for k in range(taps):
            start = PAD + half - k
            out = out + lax.dot_general(
                padded[start : start + steps, cols].astype(BF16), wd_ref[k, p], NT, preferred_element_type=F32
            )
        out_ref[:, cols] = out.astype(BF16)


def conv_backward(sel, acc, deriv, wd, pieces, micro, back_all, grad_all):
    steps, chans = acc.shape
    count = len(pieces)
    first = back_all is None
    whole = lambda shape: pl.BlockSpec(shape, lambda i, sel: (0,) * len(shape))
    any_spec = pl.BlockSpec(memory_space=pl.ANY)
    args = (sel, acc, deriv, wd, *pieces) + (() if first else (back_all, grad_all))
    n_in = len(args)
    return pl.pallas_call(
        lambda *refs: back_kernel(first, count, *refs),
        grid_spec=pltpu.PrefetchScalarGridSpec(
            num_scalar_prefetch=1,
            grid=(1,),
            in_specs=[whole((steps, chans))] * 2
            + [whole(wd.shape)]
            + [whole((steps, chans))] * count
            + ([] if first else [any_spec] * 2),
            out_specs=[
                whole((steps, chans)),
                pl.BlockSpec((1, count, steps, chans), lambda i, sel: (sel[0], 0, 0, 0)),
                pl.BlockSpec((1, steps, chans), lambda i, sel: (sel[0], 0, 0)),
            ],
            scratch_shapes=[pltpu.VMEM((steps + 2 * PAD, chans), F32)],
        ),
        out_shape=[
            jax.ShapeDtypeStruct((steps, chans), BF16),
            jax.ShapeDtypeStruct((micro + 1, count, steps, chans), BF16),
            jax.ShapeDtypeStruct((micro + 1, steps, chans), BF16),
        ],
        input_output_aliases={} if first else {n_in - 2: 1, n_in - 1: 2},
        compiler_params=params(40),
        cost_estimate=cost(2 * steps * chans * wd.shape[2] * wd.shape[0], 2 * wd.size),
        name="conv_backward",
    )(*args)


def point_grad_kernel(place_ref, act_ref, back_ref, out_ref, turned):
    @pl.when(pl.program_id(0) == 0)
    def _():
        for m in range(act_ref.shape[0]):
            steps = act_ref.shape[1]
            turned[:, m * steps : (m + 1) * steps] = act_ref[m].astype(F32).T.astype(BF16)

    micro, unused, steps, chans = back_ref.shape
    back = back_ref[...].reshape(micro * steps, chans)
    out_ref[0] = jnp.dot(turned[...], back, preferred_element_type=F32)


def point_grad(place, act_all, back_all, micro, columns):
    unused, count, steps, chans = back_all.shape
    return pl.pallas_call(
        point_grad_kernel,
        grid_spec=pltpu.PrefetchScalarGridSpec(
            num_scalar_prefetch=1,
            grid=(count,),
            in_specs=[
                pl.BlockSpec((micro, steps, chans), lambda i, place: (0, 0, 0)),
                pl.BlockSpec((micro, 1, steps, chans), lambda i, place: (0, i, 0, 0)),
            ],
            out_specs=pl.BlockSpec((1, chans, chans), lambda i, place: (0, 0, place[i])),
            scratch_shapes=[pltpu.VMEM((chans, micro * steps), BF16)],
        ),
        out_shape=jax.ShapeDtypeStruct((1, chans, columns), F32),
        compiler_params=params(40),
        cost_estimate=cost(2 * micro * steps * chans * columns, 4 * chans * columns + 2 * micro * steps * columns),
        name="point_grad",
    )(place, act_all, back_all)


def conv_grad_kernel(taps, width, pack, state_ref, grad_ref, out_ref, padded):
    micro, steps, chans = state_ref.shape
    half = taps // 2
    span = steps + 2 * PAD
    for m in range(micro):
        padded[m * span : m * span + PAD, :] = jnp.zeros((PAD, chans), F32)
        padded[m * span + PAD : m * span + PAD + steps, :] = grad_ref[m].astype(F32)
        padded[m * span + PAD + steps : (m + 1) * span, :] = jnp.zeros((PAD, chans), F32)
    lane = lax.broadcasted_iota(jnp.int32, (width, pack), 1) // width
    for p in range(chans // pack):
        cols = slice(p * pack, (p + 1) * pack)
        turned = jnp.concatenate([state_ref[m, :, cols].astype(F32).T.astype(BF16) for m in range(micro)], axis=1)
        for k in range(taps):
            start = PAD + half - k
            shifted = jnp.concatenate(
                [padded[m * span + start : m * span + start + steps, cols].astype(BF16) for m in range(micro)], axis=0
            )
            full = jnp.dot(turned, shifted, preferred_element_type=F32)
            out = jnp.zeros((width, pack), F32)
            for g in range(pack // width):
                out = jnp.where(lane == g, full[g * width : (g + 1) * width], out)
            out_ref[0, k, :, cols] = out


def conv_grad(state_all, grad_all, micro, taps, width, pack):
    unused, steps, chans = state_all.shape
    whole = pl.BlockSpec((micro, steps, chans), lambda i: (0, 0, 0))
    return pl.pallas_call(
        lambda *refs: conv_grad_kernel(taps, width, pack, *refs),
        grid=(1,),
        in_specs=[whole, whole],
        out_specs=pl.BlockSpec((1, taps, width, chans), lambda i: (0, 0, 0, 0)),
        out_shape=jax.ShapeDtypeStruct((1, taps, width, chans), F32),
        scratch_shapes=[pltpu.VMEM((micro * (steps + 2 * PAD), chans), F32)],
        compiler_params=params(40),
        cost_estimate=cost(2 * micro * steps * chans * pack * taps, 4 * micro * steps * chans),
        name="conv_grad",
    )(state_all, grad_all)


def local(inputs, labels, conv_weight, point_weight, head_weight):
    micro, steps, chans = inputs.shape
    unused, taps, width, unused_chans = conv_weight.shape
    pack = min(256, chans)
    section = lax.axis_index("section")
    n_section = lax.axis_size("section")
    last = n_section - 1
    n_chan = lax.axis_size("chan")
    chips = n_chan // 2
    chan = lax.axis_index("chan")
    chip, parity = chan // 2, chan % 2
    rounds = micro + n_section - 1

    def across(value, bits):
        return lax.ppermute(value, "chan", [(i, i ^ bits) for i in range(n_chan)])

    def along(value, step):
        pairs = [(i, i + step) for i in range(n_section) if 0 <= i + step < n_section]
        return lax.ppermute(value, "section", pairs)

    wd = block_diagonal(conv_weight[0], pack)
    weights = point_weight[0]
    own, other = [], []
    for k in range(chips):
        base = (chip ^ k) * 2
        own.append(lax.dynamic_slice_in_dim(weights, (base + parity) * chans, chans, 1))
        other.append(lax.dynamic_slice_in_dim(weights, (base + 1 - parity) * chans, chans, 1))
    twin = [across(w, 1) for w in other]
    head_rows = jnp.pad(head_weight.T, ((0, CROWS - CLASSES), (0, 0)))

    order = sorted(range(1, chips), key=lambda k: -bin(k).count("1"))
    zero = jnp.zeros((steps, chans), BF16)
    derivs = []
    act_all = state_all = None
    scores = {}

    def forward(r, recv):
        nonlocal act_all, state_all
        index = r - section
        slot = jnp.where((index >= 0) & (index < micro), index, micro)
        sel = jnp.stack([slot, section]).astype(jnp.int32)
        fresh = inputs[min(r, micro - 1)]
        state, act, deriv, act_all, state_all = conv_forward(sel, fresh, recv, wd, micro, act_all, state_all)
        derivs.append(deriv)
        act_twin = across(act, 1)
        arrived = {}
        for k in order:
            arrived[k] = across(mix(act, act_twin, own[k], twin[k]), 2 * k)
        mine = mix(act, act_twin, own[0], twin[0], state)
        parts = [arrived[k] for k in range(1, chips)]
        if r >= last:
            state, score = sum_state(mine, parts, head_rows)
            score = score + across(score, 1)
            scores[r - last] = score + sum(across(score, 2 * k) for k in range(1, chips))
        else:
            (state,) = sum_state(mine, parts)
        return along(state, 1) if r + 1 < rounds else None

    back_all = grad_all = None

    def backward(r, recv):
        nonlocal back_all, grad_all
        index = r - (last - section)
        slot = jnp.where((index >= 0) & (index < micro), index, micro)
        sel = jnp.stack([slot, section, (section == last).astype(jnp.int32)]).astype(jnp.int32)
        if r < micro:
            back = top_back(sel, scores[r], labels[r][None, :], head_rows, recv, LOSS_SCALE / (micro * steps))
        else:
            back = recv
        deriv = derivs[0]
        for s in range(n_section):
            saved = r - (last - s) + s
            if 0 <= saved < rounds:
                deriv = jnp.where(section == s, derivs[saved], deriv)
        pieces = {0: back}
        for k in order:
            pieces[k] = across(back, 2 * k)
        twins = {k: across(pieces[k], 1) for k in [0] + order[::-1]}
        acc = None
        for k in [0] + order[::-1]:
            acc = fold(acc, [(pieces[k], own[k]), (twins[k], other[k])])
        listed = [p for k in range(chips) for p in (pieces[k], twins[k])]
        back, back_all, grad_all = conv_backward(sel, acc, deriv, wd, listed, micro, back_all, grad_all)
        return along(back, -1) if r + 1 < rounds else None

    ahead, behind = zero, zero
    for t in range(rounds + n_section):
        if t < rounds:
            ahead_next = forward(t, ahead)
        if t >= n_section:
            behind = backward(t - n_section, behind)
        ahead = ahead_next

    place = jnp.stack([(chip ^ k) * 2 + (parity ^ p) for k in range(chips) for p in range(2)]).astype(jnp.int32)
    grad_point = point_grad(place, act_all, back_all, micro, point_weight.shape[2])
    grad_conv = conv_grad(state_all, grad_all, micro, taps, width, pack)
    return grad_point, grad_conv


def solution(mesh):
    placed = (
        P(None, None, "chan"),
        P(),
        P("section", None, None, "chan"),
        P("section", "chan", None),
        P("chan", None),
    )
    return jax.shard_map(
        local,
        mesh=mesh,
        in_specs=placed,
        out_specs=(P("section", "chan", None), P("section", None, None, "chan")),
        check_vma=False,
    )
```

```python
import jax
import jax.numpy as jnp
from jax import lax
from jax.experimental import pallas as pl
from jax.experimental.pallas import tpu as pltpu
from jax.sharding import PartitionSpec as P

CLASSES = 3
LOSS_SCALE = 2048
CROWS = 8
PAD = 8
F32 = jnp.float32
BF16 = jnp.bfloat16
NT = (((1,), (1,)), ((), ()))
TN = (((0,), (0,)), ((), ()))


def params(mib):
    return pltpu.CompilerParams(vmem_limit_bytes=mib * 1024 * 1024)


def cost(flops, moved):
    return pl.CostEstimate(flops=int(flops), bytes_accessed=int(moved), transcendentals=0)


def vmem_spec():
    return pl.BlockSpec(memory_space=pltpu.VMEM)


def smem_spec():
    return pl.BlockSpec(memory_space=pltpu.SMEM)


def block_diagonal(kernel, pack):
    taps, width, chans = kernel.shape
    shaped = jnp.transpose(kernel.reshape(taps, width, chans // pack, pack), (0, 2, 1, 3))
    tiled = jnp.tile(shaped, (1, 1, pack // width, 1))
    row = jnp.arange(pack)[:, None] // width
    col = jnp.arange(pack)[None, :] // width
    return jnp.where(row == col, tiled, jnp.zeros_like(tiled))


def fill_padded(padded, field):
    steps, chans = field.shape
    padded[0:PAD, :] = jnp.zeros((PAD, chans), F32)
    padded[PAD : PAD + steps, :] = field
    padded[PAD + steps : PAD + steps + PAD, :] = jnp.zeros((PAD, chans), F32)


def slot_of(index, micro):
    return jnp.where((index >= 0) & (index < micro), index, micro)


def in_hbm(arrays):
    return [pltpu.with_memory_space_constraint(a, pltpu.HBM) for a in arrays]


def in_vmem(array):
    return pltpu.with_memory_space_constraint(array, pltpu.VMEM)


def hbm_spec():
    return pl.BlockSpec(memory_space=pltpu.HBM)


def split_kernel(place_ref, weights, own_ref, other_ref, sems):
    chips, unused, chans = own_ref.shape
    copies = []
    for k in range(chips):
        for i, target in enumerate((own_ref, other_ref)):
            start = pl.multiple_of(place_ref[2 * k + i] * chans, 128)
            copies.append(pltpu.make_async_copy(weights.at[:, pl.ds(start, chans)], target.at[k], sems.at[i, k]))
    for copy in copies:
        copy.start()
    for copy in copies:
        copy.wait()


def split(place, weights, chips):
    rows = weights.shape[0]
    one = jax.ShapeDtypeStruct((chips, rows, rows), weights.dtype)
    return pl.pallas_call(
        split_kernel,
        in_specs=[smem_spec(), hbm_spec()],
        out_specs=[vmem_spec()] * 2,
        out_shape=[one, one],
        scratch_shapes=[pltpu.SemaphoreType.DMA((2, chips))],
        compiler_params=params(8),
        cost_estimate=cost(0, 4 * weights.size),
        name="split",
    )(place, *in_hbm([weights]))


def load_kernel(source, out_ref, sems):
    chips = out_ref.shape[0]
    copies = [pltpu.make_async_copy(source.at[k], out_ref.at[k], sems.at[k]) for k in range(chips)]
    for copy in copies:
        copy.start()
    for copy in copies:
        copy.wait()


def load(array):
    return pl.pallas_call(
        load_kernel,
        in_specs=[hbm_spec()],
        out_specs=vmem_spec(),
        out_shape=jax.ShapeDtypeStruct(array.shape, array.dtype),
        scratch_shapes=[pltpu.SemaphoreType.DMA((array.shape[0],))],
        compiler_params=params(8),
        cost_estimate=cost(0, 4 * array.size),
        name="load",
    )(*in_hbm([array]))


def turn_kernel(source, out_ref):
    for k in range(out_ref.shape[0]):
        out_ref[k] = source[k].astype(F32).T.astype(BF16)


def turn(array):
    count, rows, columns = array.shape
    return pl.pallas_call(
        turn_kernel,
        in_specs=[vmem_spec()],
        out_specs=vmem_spec(),
        out_shape=jax.ShapeDtypeStruct((count, columns, rows), BF16),
        compiler_params=params(8),
        cost_estimate=cost(0, 4 * array.size),
        name="turn",
    )(array)


def conv_kernel(info_ref, fresh_ref, recv_ref, wd_ref, state_ref, act_ref, deriv_ref, padded):
    taps, packs, pack, unused = wd_ref.shape
    steps, chans = fresh_ref.shape
    half = taps // 2
    state = jnp.where(info_ref[0] == 0, fresh_ref[...], recv_ref[...])
    state_ref[...] = state
    fill_padded(padded, state.astype(F32))
    for p in range(packs):
        cols = slice(p * pack, (p + 1) * pack)
        out = jnp.zeros((steps, pack), F32)
        for k in range(taps):
            start = PAD + k - half
            out = out + jnp.dot(
                padded[start : start + steps, cols].astype(BF16), wd_ref[k, p], preferred_element_type=F32
            )
        sig = jax.nn.sigmoid(out)
        act_ref[:, cols] = (out * sig).astype(BF16)
        deriv_ref[:, cols] = sig * (1.0 + out * (1.0 - sig))


def conv_forward(info, fresh, recv, wd):
    steps, chans = fresh.shape
    one = jax.ShapeDtypeStruct((steps, chans), BF16)
    return pl.pallas_call(
        conv_kernel,
        in_specs=[smem_spec()] + [vmem_spec()] * 3,
        out_specs=[vmem_spec()] * 3,
        out_shape=[one, one, jax.ShapeDtypeStruct((steps, chans), F32)],
        scratch_shapes=[pltpu.VMEM((steps + 2 * PAD, chans), F32)],
        compiler_params=params(12),
        cost_estimate=cost(2 * steps * chans * wd.shape[2] * wd.shape[0], 2 * wd.size),
        name="conv_forward",
    )(info, fresh, recv, in_vmem(wd))


def mix_kernel(k, a_ref, b_ref, wa_ref, wb_ref, out_ref):
    total = jnp.dot(a_ref[...], wa_ref[k], preferred_element_type=F32)
    total = total + jnp.dot(b_ref[...], wb_ref[k], preferred_element_type=F32)
    out_ref[...] = total.astype(out_ref.dtype)


def mix(act, act_twin, wa, wb, k):
    steps, chans = act.shape
    return pl.pallas_call(
        lambda *refs: mix_kernel(k, *refs),
        in_specs=[vmem_spec()] * 4,
        out_specs=vmem_spec(),
        out_shape=jax.ShapeDtypeStruct((steps, wa.shape[2]), BF16),
        compiler_params=params(8),
        cost_estimate=cost(4 * steps * chans * wa.shape[2], 4 * wa[0].size),
        name="mix",
    )(act, act_twin, in_vmem(wa), in_vmem(wb))


def mix_own_kernel(r, info_ref, a_ref, b_ref, wa_ref, wb_ref, state_ref, deriv_ref, *refs):
    out_ref, act_all, state_all, deriv_all, sems = refs[-5:]
    k, slot = 0, slot_of(r - info_ref[0], act_all.shape[0] - 1)
    copies = [
        pltpu.make_async_copy(a_ref, act_all.at[slot], sems.at[0]),
        pltpu.make_async_copy(state_ref, state_all.at[slot], sems.at[1]),
        pltpu.make_async_copy(deriv_ref, deriv_all.at[slot], sems.at[2]),
    ]
    for copy in copies:
        copy.start()
    total = jnp.dot(a_ref[...], wa_ref[k], preferred_element_type=F32)
    total = total + jnp.dot(b_ref[...], wb_ref[k], preferred_element_type=F32)
    out_ref[...] = total + state_ref[...].astype(F32)
    for copy in copies:
        copy.wait()


def mix_own(r, info, act, act_twin, wa, wb, state, deriv, stored, micro):
    steps, chans = act.shape
    full = (micro + 1, steps, chans)
    return pl.pallas_call(
        lambda *refs: mix_own_kernel(r, *refs),
        in_specs=[smem_spec()] + [vmem_spec()] * 6 + [hbm_spec()] * len(stored),
        out_specs=[vmem_spec()] + [hbm_spec()] * 3,
        out_shape=[
            jax.ShapeDtypeStruct((steps, chans), F32),
            pltpu.HBM(full, BF16),
            pltpu.HBM(full, BF16),
            pltpu.HBM(full, F32),
        ],
        input_output_aliases={7: 1, 8: 2, 9: 3} if stored else {},
        scratch_shapes=[pltpu.SemaphoreType.DMA((3,))],
        compiler_params=params(8),
        cost_estimate=cost(4 * steps * chans * wa.shape[2], 4 * wa[0].size),
        name="mix_own",
    )(info, act, act_twin, in_vmem(wa), in_vmem(wb), state, deriv, *in_hbm(stored))


def sum_kernel(with_head, own_ref, *refs):
    if with_head:
        *parts, head_ref, out_ref, score_ref = refs
    else:
        *parts, out_ref = refs
    total = own_ref[...]
    for part in parts:
        total = total + part[...].astype(F32)
    state = total.astype(BF16)
    out_ref[...] = state
    if with_head:
        score_ref[...] = lax.dot_general(head_ref[...], state, NT, preferred_element_type=F32)


def sum_state(own, parts, head_rows=None):
    steps, chans = own.shape
    args = (own, *parts) + (() if head_rows is None else (head_rows,))
    shapes = [jax.ShapeDtypeStruct((steps, chans), BF16)]
    if head_rows is not None:
        shapes.append(jax.ShapeDtypeStruct((CROWS, steps), F32))
    return pl.pallas_call(
        lambda *refs: sum_kernel(head_rows is not None, *refs),
        in_specs=[vmem_spec()] * len(args),
        out_specs=[vmem_spec()] * len(shapes),
        out_shape=shapes,
        compiler_params=params(8),
        cost_estimate=cost(steps * chans * 8, 8 * steps * chans),
        name="sum_state",
    )(*args)


def top_kernel(scale, score_ref, label_ref, head_ref, out_ref):
    score = score_ref[...]
    row = lax.broadcasted_iota(jnp.int32, score.shape, 0)
    hot = (label_ref[...] == row).astype(F32)
    top = (jax.nn.sigmoid(score) - hot) * scale
    top = jnp.where(row < CLASSES, top, 0.0)
    out_ref[...] = lax.dot_general(
        top, head_ref[...].astype(F32), TN, preferred_element_type=F32, precision=lax.Precision.HIGHEST
    ).astype(BF16)


def top_back(score, label_row, head_rows, scale):
    return pl.pallas_call(
        lambda *refs: top_kernel(scale, *refs),
        in_specs=[vmem_spec()] * 3,
        out_specs=vmem_spec(),
        out_shape=jax.ShapeDtypeStruct((score.shape[1], head_rows.shape[1]), BF16),
        compiler_params=params(8),
        name="top_back",
    )(score, label_row, head_rows)


def choose_kernel(info_ref, top_ref, recv_ref, out_ref):
    out_ref[...] = jnp.where(info_ref[0] == info_ref[1], top_ref[...], recv_ref[...])


def choose(info, top, recv):
    return pl.pallas_call(
        choose_kernel,
        in_specs=[smem_spec()] + [vmem_spec()] * 2,
        out_specs=vmem_spec(),
        out_shape=jax.ShapeDtypeStruct(recv.shape, BF16),
        compiler_params=params(8),
        cost_estimate=cost(0, 4 * recv.size),
        name="choose",
    )(info, top, recv)


def fold_terms(total, piece_refs, weight_refs, terms):
    for piece, (array, k) in zip(piece_refs, terms):
        part = jnp.dot(piece[...], weight_refs[array][k], preferred_element_type=F32)
        total = part if total is None else total + part
    return total


def fold_kernel(r, terms, places, info_ref, *refs):
    out_ref, back_all, sems = refs[-3:]
    count = len(terms)
    pieces = refs[:count]
    slot = slot_of(r - (info_ref[1] - info_ref[0]), back_all.shape[0] - 1)
    copies = [pltpu.make_async_copy(pieces[i], back_all.at[slot, places[i]], sems.at[i]) for i in range(count)]
    for copy in copies:
        copy.start()
    out_ref[...] = fold_terms(None, pieces, refs[count : count + 2], terms)
    for copy in copies:
        copy.wait()


def fold(r, info, pieces, weights, terms, places, micro, stored):
    steps, rows = pieces[0].shape[0], weights[0].shape[2]
    args = (info, *pieces, *[in_vmem(w) for w in weights])
    n = len(args)
    return pl.pallas_call(
        lambda *refs: fold_kernel(r, terms, places, *refs),
        in_specs=[smem_spec()] + [vmem_spec()] * (n - 1) + [hbm_spec()] * len(stored),
        out_specs=[vmem_spec(), hbm_spec()],
        out_shape=[
            jax.ShapeDtypeStruct((steps, rows), F32),
            pltpu.HBM((micro + 1, 2 * weights[0].shape[0], *pieces[0].shape), BF16),
        ],
        input_output_aliases={n: 1} if stored else {},
        scratch_shapes=[pltpu.SemaphoreType.DMA((len(pieces),))],
        compiler_params=params(8),
        cost_estimate=cost(2 * pieces[0].size * rows * len(terms), 2 * rows * rows * len(terms)),
        name="fold",
    )(*args, *in_hbm(stored))


def back_kernel(r, terms, places, onward, info_ref, acc_ref, wd_ref, back_ref, weight_ref, *refs):
    piece_refs = refs[: len(terms)]
    deriv_all = refs[len(terms)]
    outs = refs[-7 if onward else -6 :]
    back_all, grad_all, padded, deriv_ref, grad_ref, sems = outs[-6:]
    taps, packs, pack, unused = wd_ref.shape
    steps, chans = acc_ref.shape
    half = taps // 2
    slot = slot_of(r - (info_ref[1] - info_ref[0]), deriv_all.shape[0] - 1)
    fetch = pltpu.make_async_copy(deriv_all.at[slot], deriv_ref, sems.at[0])
    fetch.start()
    copies = [
        pltpu.make_async_copy(piece_refs[i], back_all.at[slot, places[i]], sems.at[2 + i]) for i in range(len(terms))
    ]
    for copy in copies:
        copy.start()
    total = fold_terms(acc_ref[...], piece_refs, [weight_ref], terms)
    fetch.wait()
    grad = (total * deriv_ref[...]).astype(BF16)
    grad_ref[...] = grad
    put = pltpu.make_async_copy(grad_ref, grad_all.at[slot], sems.at[1])
    put.start()
    if onward:
        out_ref = outs[0]
        fill_padded(padded, grad.astype(F32))
        for p in range(packs):
            cols = slice(p * pack, (p + 1) * pack)
            out = back_ref[:, cols].astype(F32)
            for k in range(taps):
                start = PAD + half - k
                out = out + jnp.dot(
                    padded[start : start + steps, cols].astype(BF16), wd_ref[k, p], preferred_element_type=F32
                )
            out_ref[:, cols] = out.astype(BF16)
    put.wait()
    for copy in copies:
        copy.wait()


def conv_backward(r, info, acc, deriv_all, wd, back, weight, pieces, terms, places, onward, back_all, stored):
    steps, chans = acc.shape
    args = (info, acc, in_vmem(wd), back, in_vmem(weight), *pieces)
    n = len(args)
    outs = 1 if onward else 0
    return pl.pallas_call(
        lambda *refs: back_kernel(r, terms, places, onward, *refs),
        in_specs=[smem_spec()] + [vmem_spec()] * (n - 1) + [hbm_spec()] * (2 + len(stored)),
        out_specs=[vmem_spec()] * outs + [hbm_spec()] * 2,
        out_shape=[jax.ShapeDtypeStruct((steps, chans), BF16)] * outs
        + [pltpu.HBM(back_all.shape, BF16), pltpu.HBM((back_all.shape[0], steps, chans), BF16)],
        input_output_aliases={n + 1: outs, n + 2: outs + 1} if stored else {n + 1: outs},
        scratch_shapes=[
            pltpu.VMEM((steps + 2 * PAD, chans), F32),
            pltpu.VMEM((steps, chans), F32),
            pltpu.VMEM((steps, chans), BF16),
            pltpu.SemaphoreType.DMA((2 + len(pieces),)),
        ],
        compiler_params=params(8),
        cost_estimate=cost(2 * steps * chans * wd.shape[2] * wd.shape[0], 2 * wd.size),
        name="conv_backward",
    )(*args, *in_hbm([deriv_all, back_all, *stored]))


def point_grad_kernel(place_ref, act_all, back_all, out_ref, acts, backs, outs, turned, act_sems, in_sems, out_sems):
    unused, count, steps, chans = back_all.shape
    micro = acts.shape[0]
    depth = backs.shape[0]
    bands = out_sems.shape[1]
    band = chans // bands

    def fetch(j):
        return [
            pltpu.make_async_copy(back_all.at[m, j], backs.at[j % depth, pl.ds(m * steps, steps), :], in_sems.at[j % depth, m])
            for m in range(micro)
        ]

    def put(j):
        start = pl.multiple_of(place_ref[j] * chans, 128)
        return [
            pltpu.make_async_copy(
                outs.at[j % depth, pl.ds(i * band, band), :],
                out_ref.at[0, pl.ds(i * band, band), pl.ds(start, chans)],
                out_sems.at[j % depth, i],
            )
            for i in range(bands)
        ]

    loads = [pltpu.make_async_copy(act_all.at[m], acts.at[m], act_sems.at[m]) for m in range(micro)]
    for copy in loads:
        copy.start()
    for j in range(min(depth - 1, count)):
        for copy in fetch(j):
            copy.start()
    for m in range(micro):
        loads[m].wait()
        turned[:, m * steps : (m + 1) * steps] = acts[m].astype(F32).T.astype(BF16)
    for j in range(count):
        if j + depth - 1 < count:
            for copy in fetch(j + depth - 1):
                copy.start()
        for copy in fetch(j):
            copy.wait()
        if j >= depth:
            for copy in put(j - depth):
                copy.wait()
        outs[j % depth] = jnp.dot(turned[...], backs[j % depth], preferred_element_type=F32)
        for copy in put(j):
            copy.start()
    for j in range(max(0, count - depth), count):
        for copy in put(j):
            copy.wait()


def point_grad(place, act_all, back_all, micro, columns):
    unused, count, steps, chans = back_all.shape
    depth = 3
    bands = 4 if chans >= 256 else 1
    return pl.pallas_call(
        point_grad_kernel,
        in_specs=[smem_spec(), hbm_spec(), hbm_spec()],
        out_specs=hbm_spec(),
        out_shape=pltpu.HBM((1, chans, columns), F32),
        scratch_shapes=[
            pltpu.VMEM((micro, steps, chans), BF16),
            pltpu.VMEM((depth, micro * steps, chans), BF16),
            pltpu.VMEM((depth, chans, chans), F32),
            pltpu.VMEM((chans, micro * steps), BF16),
            pltpu.SemaphoreType.DMA((micro,)),
            pltpu.SemaphoreType.DMA((depth, micro)),
            pltpu.SemaphoreType.DMA((depth, bands)),
        ],
        compiler_params=params(20),
        cost_estimate=cost(2 * micro * steps * chans * columns, 4 * chans * columns + 2 * micro * steps * columns),
        name="point_grad",
    )(place, *in_hbm([act_all, back_all]))


def conv_grad_kernel(taps, width, pack, state_ref, grad_ref, out_ref, padded):
    micro, steps, chans = state_ref.shape
    half = taps // 2
    span = steps + 2 * PAD
    for m in range(micro):
        padded[m * span : m * span + PAD, :] = jnp.zeros((PAD, chans), F32)
        padded[m * span + PAD : m * span + PAD + steps, :] = grad_ref[m].astype(F32)
        padded[m * span + PAD + steps : (m + 1) * span, :] = jnp.zeros((PAD, chans), F32)
    lane = lax.broadcasted_iota(jnp.int32, (width, pack), 1) // width
    for p in range(chans // pack):
        cols = slice(p * pack, (p + 1) * pack)
        turned = jnp.concatenate([state_ref[m, :, cols].astype(F32).T.astype(BF16) for m in range(micro)], axis=1)
        for k in range(taps):
            start = PAD + half - k
            shifted = jnp.concatenate(
                [padded[m * span + start : m * span + start + steps, cols].astype(BF16) for m in range(micro)], axis=0
            )
            full = jnp.dot(turned, shifted, preferred_element_type=F32)
            out = jnp.zeros((width, pack), F32)
            for g in range(pack // width):
                out = jnp.where(lane == g, full[g * width : (g + 1) * width], out)
            out_ref[0, k, :, cols] = out


def conv_grad(state_all, grad_all, micro, taps, width, pack):
    unused, steps, chans = state_all.shape
    whole = pl.BlockSpec((micro, steps, chans), lambda i: (0, 0, 0))
    return pl.pallas_call(
        lambda *refs: conv_grad_kernel(taps, width, pack, *refs),
        grid=(1,),
        in_specs=[whole, whole],
        out_specs=pl.BlockSpec((1, taps, width, chans), lambda i: (0, 0, 0, 0)),
        out_shape=jax.ShapeDtypeStruct((1, taps, width, chans), F32),
        scratch_shapes=[pltpu.VMEM((micro * (steps + 2 * PAD), chans), F32)],
        compiler_params=params(20),
        cost_estimate=cost(2 * micro * steps * chans * pack * taps, 4 * micro * steps * chans),
        name="conv_grad",
    )(*in_hbm([state_all, grad_all]))


def local(inputs, labels, conv_weight, point_weight, head_weight):
    micro, steps, chans = inputs.shape
    unused, taps, width, unused_chans = conv_weight.shape
    pack = min(256, chans)
    section = lax.axis_index("section")
    n_section = lax.axis_size("section")
    last = n_section - 1
    n_chan = lax.axis_size("chan")
    chips = n_chan // 2
    chan = lax.axis_index("chan")
    chip, parity = chan // 2, chan % 2
    rounds = micro + n_section - 1

    def across(value, bits):
        return lax.ppermute(value, "chan", [(i, i ^ bits) for i in range(n_chan)])

    def along(value, step):
        pairs = [(i, i + step) for i in range(n_section) if 0 <= i + step < n_section]
        return lax.ppermute(value, "section", pairs)

    wd = block_diagonal(conv_weight[0], pack)
    weights = point_weight[0]
    place = jnp.stack([(chip ^ k) * 2 + (parity ^ p) for k in range(chips) for p in range(2)]).astype(jnp.int32)
    own, other = split(place, weights, chips)
    twin = load(across(other, 1))
    own_turned, other_turned = turn(own), turn(other)
    wd_turned = turn(wd.reshape(-1, pack, pack)).reshape(wd.shape)
    head_rows = jnp.pad(head_weight.T, ((0, CROWS - CLASSES), (0, 0)))

    order = sorted(range(1, chips), key=lambda k: -bin(k).count("1"))
    info = jnp.stack([section, jnp.int32(last)]).astype(jnp.int32)
    zero = jnp.zeros((steps, chans), BF16)
    kept, gone = [], []
    scores = {}

    def forward(r, recv):
        nonlocal kept
        state, act, deriv = conv_forward(info, inputs[min(r, micro - 1)], recv, wd)
        act_twin = across(act, 1)
        arrived = {}
        for k in order:
            arrived[k] = across(mix(act, act_twin, own, twin, k), 2 * k)
        mine, *kept = mix_own(r, info, act, act_twin, own, twin, state, deriv, kept, micro)
        parts = [arrived[k] for k in range(1, chips)]
        if r >= last:
            state, score = sum_state(mine, parts, head_rows)
            score = score + across(score, 1)
            scores[r - last] = score + sum(across(score, 2 * k) for k in range(1, chips))
        else:
            (state,) = sum_state(mine, parts)
        return along(state, 1) if r + 1 < rounds else None

    def backward(r, recv):
        nonlocal gone
        back = recv
        if r < micro:
            top = top_back(scores[r], labels[r][None, :], head_rows, LOSS_SCALE / (micro * steps))
            back = choose(info, top, recv)
        pieces = {0: back}
        for k in order:
            pieces[k] = across(back, 2 * k)
        rest = list(range(1, chips))
        twins = {0: across(back, 1)}
        twins.update({k: across(pieces[k], 1) for k in rest})
        onward = r + 1 < rounds
        terms = [(1, 0)] + [(0, k) for k in range(chips)]
        places = [1] + [2 * k for k in range(chips)]
        listed = [twins[0]] + [pieces[k] for k in range(chips)]
        acc, back_all = fold(r, info, listed, [own_turned, other_turned], terms, places, micro, gone[:1])
        terms, places = [(0, k) for k in rest], [2 * k + 1 for k in rest]
        listed = [twins[k] for k in rest]
        *back, back_all, grad_all = conv_backward(
            r, info, acc, kept[2], wd_turned, back, other_turned, listed, terms, places, onward, back_all, gone[1:]
        )
        gone = [back_all, grad_all]
        return along(back[0], -1) if onward else None

    ahead, behind = zero, zero
    for t in range(rounds + n_section):
        if t < rounds:
            ahead_next = forward(t, ahead)
        if t >= n_section:
            behind = backward(t - n_section, behind)
        ahead = ahead_next

    grad_point = point_grad(place, kept[0], gone[0], micro, point_weight.shape[2])
    grad_conv = conv_grad(kept[1], gone[1], micro, taps, width, pack)
    return grad_point, grad_conv


def solution(mesh):
    placed = (
        P(None, None, "chan"),
        P(),
        P("section", None, None, "chan"),
        P("section", "chan", None),
        P("chan", None),
    )
    return jax.shard_map(
        local,
        mesh=mesh,
        in_specs=placed,
        out_specs=(P("section", "chan", None), P("section", None, None, "chan")),
        check_vma=False,
    )
```

```python
import jax
import jax.numpy as jnp
from jax import lax
from jax.experimental import pallas as pl
from jax.experimental.pallas import tpu as pltpu
from jax.sharding import PartitionSpec as P

CLASSES = 3
LOSS_SCALE = 2048
CROWS = 8
PAD = 8
F32 = jnp.float32
BF16 = jnp.bfloat16
NT = (((1,), (1,)), ((), ()))
TN = (((0,), (0,)), ((), ()))


def params(mib):
    return pltpu.CompilerParams(vmem_limit_bytes=mib * 1024 * 1024)


def cost(flops, moved):
    return pl.CostEstimate(flops=int(flops), bytes_accessed=int(moved), transcendentals=0)


def vmem_spec():
    return pl.BlockSpec(memory_space=pltpu.VMEM)


def smem_spec():
    return pl.BlockSpec(memory_space=pltpu.SMEM)


def block_diagonal(kernel, pack):
    taps, width, chans = kernel.shape
    shaped = jnp.transpose(kernel.reshape(taps, width, chans // pack, pack), (0, 2, 1, 3))
    tiled = jnp.tile(shaped, (1, 1, pack // width, 1))
    row = jnp.arange(pack)[:, None] // width
    col = jnp.arange(pack)[None, :] // width
    return jnp.where(row == col, tiled, jnp.zeros_like(tiled))


def fill_padded(padded, field):
    steps, chans = field.shape
    padded[0:PAD, :] = jnp.zeros((PAD, chans), F32)
    padded[PAD : PAD + steps, :] = field
    padded[PAD + steps : PAD + steps + PAD, :] = jnp.zeros((PAD, chans), F32)


def slot_of(index, micro):
    return jnp.where((index >= 0) & (index < micro), index, micro)


def in_hbm(arrays):
    return [pltpu.with_memory_space_constraint(a, pltpu.HBM) for a in arrays]


def in_vmem(array):
    return pltpu.with_memory_space_constraint(array, pltpu.VMEM)


def hbm_spec():
    return pl.BlockSpec(memory_space=pltpu.HBM)


def split_kernel(place_ref, weights, own_ref, other_ref, sems):
    chips, unused, chans = own_ref.shape
    copies = []
    for k in range(chips):
        for i, target in enumerate((own_ref, other_ref)):
            start = pl.multiple_of(place_ref[2 * k + i] * chans, 128)
            copies.append(pltpu.make_async_copy(weights.at[:, pl.ds(start, chans)], target.at[k], sems.at[i, k]))
    for copy in copies:
        copy.start()
    for copy in copies:
        copy.wait()


def split(place, weights, chips):
    rows = weights.shape[0]
    one = jax.ShapeDtypeStruct((chips, rows, rows), weights.dtype)
    return pl.pallas_call(
        split_kernel,
        in_specs=[smem_spec(), hbm_spec()],
        out_specs=[vmem_spec()] * 2,
        out_shape=[one, one],
        scratch_shapes=[pltpu.SemaphoreType.DMA((2, chips))],
        compiler_params=params(8),
        cost_estimate=cost(0, 4 * weights.size),
        name="split",
    )(place, *in_hbm([weights]))


def load_kernel(source, out_ref, sems):
    chips = out_ref.shape[0]
    copies = [pltpu.make_async_copy(source.at[k], out_ref.at[k], sems.at[k]) for k in range(chips)]
    for copy in copies:
        copy.start()
    for copy in copies:
        copy.wait()


def load(array):
    return pl.pallas_call(
        load_kernel,
        in_specs=[hbm_spec()],
        out_specs=vmem_spec(),
        out_shape=jax.ShapeDtypeStruct(array.shape, array.dtype),
        scratch_shapes=[pltpu.SemaphoreType.DMA((array.shape[0],))],
        compiler_params=params(8),
        cost_estimate=cost(0, 4 * array.size),
        name="load",
    )(*in_hbm([array]))


def turn_weights_kernel(source, *refs):
    out_ref, mark_ref = refs[-2:]
    mark_ref[...] = jnp.zeros_like(mark_ref)
    for k in range(out_ref.shape[0]):
        out_ref[k] = source[k].astype(F32).T.astype(BF16)


def turn(array, after):
    count, rows, columns = array.shape
    return pl.pallas_call(
        turn_weights_kernel,
        in_specs=[vmem_spec()] * (1 + len(after)),
        out_specs=[vmem_spec()] * 2,
        out_shape=[jax.ShapeDtypeStruct((count, columns, rows), BF16), jax.ShapeDtypeStruct((8, 128), F32)],
        compiler_params=params(8),
        cost_estimate=cost(0, 4 * array.size),
        name="turn",
    )(array, *after)


def conv_kernel(info_ref, fresh_ref, recv_ref, wd_ref, state_ref, act_ref, deriv_ref, padded):
    taps, packs, pack, unused = wd_ref.shape
    steps, chans = fresh_ref.shape
    half = taps // 2
    state = jnp.where(info_ref[0] == 0, fresh_ref[...], recv_ref[...])
    state_ref[...] = state
    fill_padded(padded, state.astype(F32))
    for p in range(packs):
        cols = slice(p * pack, (p + 1) * pack)
        out = jnp.zeros((steps, pack), F32)
        for k in range(taps):
            start = PAD + k - half
            out = out + jnp.dot(
                padded[start : start + steps, cols].astype(BF16), wd_ref[k, p], preferred_element_type=F32
            )
        sig = jax.nn.sigmoid(out)
        act_ref[:, cols] = (out * sig).astype(BF16)
        deriv_ref[:, cols] = sig * (1.0 + out * (1.0 - sig))


def conv_forward(info, fresh, recv, wd):
    steps, chans = fresh.shape
    one = jax.ShapeDtypeStruct((steps, chans), BF16)
    return pl.pallas_call(
        conv_kernel,
        in_specs=[smem_spec()] + [vmem_spec()] * 3,
        out_specs=[vmem_spec()] * 3,
        out_shape=[one, one, jax.ShapeDtypeStruct((steps, chans), F32)],
        scratch_shapes=[pltpu.VMEM((steps + 2 * PAD, chans), F32)],
        compiler_params=params(12),
        cost_estimate=cost(2 * steps * chans * wd.shape[2] * wd.shape[0], 2 * wd.size),
        name="conv_forward",
    )(info, fresh, recv, in_vmem(wd))


def scored(head_ref, k, total, before_ref):
    high = total.astype(BF16)
    low = (total - high.astype(F32)).astype(BF16)
    score = lax.dot_general(head_ref[k], high, NT, preferred_element_type=F32)
    score = score + lax.dot_general(head_ref[k], low, NT, preferred_element_type=F32)
    return score if before_ref is None else score + before_ref[...]


def mix_kernel(k, head, before, a_ref, b_ref, wa_ref, wb_ref, *refs):
    total = jnp.dot(a_ref[...], wa_ref[k], preferred_element_type=F32)
    total = total + jnp.dot(b_ref[...], wb_ref[k], preferred_element_type=F32)
    if not head:
        refs[-1][...] = total.astype(BF16)
        return
    out_ref, score_ref = refs[-2:]
    sent = total.astype(BF16)
    out_ref[...] = sent
    score_ref[...] = scored(refs[0], k, sent.astype(F32), refs[1] if before else None)


def mix(act, act_twin, wa, wb, k, heads=None, before=None):
    steps, chans = act.shape
    args = (act, act_twin, in_vmem(wa), in_vmem(wb)) + (() if heads is None else (heads,))
    args = args + (() if before is None else (before,))
    shapes = [jax.ShapeDtypeStruct((steps, wa.shape[2]), BF16)]
    if heads is not None:
        shapes.append(jax.ShapeDtypeStruct((CROWS, steps), F32))
    return pl.pallas_call(
        lambda *refs: mix_kernel(k, heads is not None, before is not None, *refs),
        in_specs=[vmem_spec()] * len(args),
        out_specs=[vmem_spec()] * len(shapes),
        out_shape=shapes,
        compiler_params=params(8),
        cost_estimate=cost(4 * steps * chans * wa.shape[2], 4 * wa[0].size),
        name="mix",
    )(*args)


def mix_own_kernel(r, head, info_ref, a_ref, b_ref, wa_ref, wb_ref, state_ref, deriv_ref, *refs):
    outs = refs[-6 if head else -5 :]
    act_all, state_all, deriv_all, sems = outs[-4:]
    k, slot = 0, slot_of(r - info_ref[0], act_all.shape[0] - 1)
    copies = [
        pltpu.make_async_copy(a_ref, act_all.at[slot], sems.at[0]),
        pltpu.make_async_copy(state_ref, state_all.at[slot], sems.at[1]),
        pltpu.make_async_copy(deriv_ref, deriv_all.at[slot], sems.at[2]),
    ]
    for copy in copies:
        copy.start()
    total = jnp.dot(a_ref[...], wa_ref[k], preferred_element_type=F32)
    total = total + jnp.dot(b_ref[...], wb_ref[k], preferred_element_type=F32)
    total = total + state_ref[...].astype(F32)
    outs[0][...] = total
    if head:
        outs[1][...] = scored(refs[0], k, total, refs[1])
    for copy in copies:
        copy.wait()


def mix_own(r, info, act, act_twin, wa, wb, state, deriv, stored, micro, heads=None, before=None):
    steps, chans = act.shape
    full = (micro + 1, steps, chans)
    args = (info, act, act_twin, in_vmem(wa), in_vmem(wb), state, deriv)
    args = args + (() if heads is None else (heads, before))
    n = len(args)
    shapes = [jax.ShapeDtypeStruct((steps, chans), F32)]
    if heads is not None:
        shapes.append(jax.ShapeDtypeStruct((CROWS, steps), F32))
    outs = len(shapes)
    return pl.pallas_call(
        lambda *refs: mix_own_kernel(r, heads is not None, *refs),
        in_specs=[smem_spec()] + [vmem_spec()] * (n - 1) + [hbm_spec()] * len(stored),
        out_specs=[vmem_spec()] * outs + [hbm_spec()] * 3,
        out_shape=shapes + [pltpu.HBM(full, BF16), pltpu.HBM(full, BF16), pltpu.HBM(full, F32)],
        input_output_aliases={n + i: outs + i for i in range(3)} if stored else {},
        scratch_shapes=[pltpu.SemaphoreType.DMA((3,))],
        compiler_params=params(8),
        cost_estimate=cost(4 * steps * chans * wa.shape[2], 4 * wa[0].size),
        name="mix_own",
    )(*args, *in_hbm(stored))


def sum_kernel(count, own_ref, *refs):
    parts, out_ref = refs[:count], refs[-1]
    total = own_ref[...]
    for part in parts:
        total = total + part[...].astype(F32)
    out_ref[...] = total.astype(BF16)


def sum_state(own, parts, after):
    steps, chans = own.shape
    return pl.pallas_call(
        lambda *refs: sum_kernel(len(parts), *refs),
        in_specs=[vmem_spec()] * (1 + len(parts) + len(after)),
        out_specs=vmem_spec(),
        out_shape=jax.ShapeDtypeStruct((steps, chans), BF16),
        compiler_params=params(8),
        cost_estimate=cost(steps * chans * 8, 8 * steps * chans),
        name="sum_state",
    )(own, *parts, *after)


def top_kernel(scale, score_ref, label_ref, head_ref, out_ref):
    score = score_ref[...]
    row = lax.broadcasted_iota(jnp.int32, score.shape, 0)
    hot = (label_ref[...] == row).astype(F32)
    top = (jax.nn.sigmoid(score) - hot) * scale
    top = jnp.where(row < CLASSES, top, 0.0)
    out_ref[...] = lax.dot_general(
        top, head_ref[...].astype(F32), TN, preferred_element_type=F32, precision=lax.Precision.HIGHEST
    ).astype(BF16)


def top_back(score, label_row, head_rows, scale):
    return pl.pallas_call(
        lambda *refs: top_kernel(scale, *refs),
        in_specs=[vmem_spec()] * 3,
        out_specs=vmem_spec(),
        out_shape=jax.ShapeDtypeStruct((score.shape[1], head_rows.shape[1]), BF16),
        compiler_params=params(8),
        name="top_back",
    )(score, label_row, head_rows)


def choose_kernel(info_ref, top_ref, recv_ref, out_ref):
    out_ref[...] = jnp.where(info_ref[0] == info_ref[1], top_ref[...], recv_ref[...])


def choose(info, top, recv):
    return pl.pallas_call(
        choose_kernel,
        in_specs=[smem_spec()] + [vmem_spec()] * 2,
        out_specs=vmem_spec(),
        out_shape=jax.ShapeDtypeStruct(recv.shape, BF16),
        compiler_params=params(8),
        cost_estimate=cost(0, 4 * recv.size),
        name="choose",
    )(info, top, recv)


def fold_terms(total, piece_refs, weight_refs, terms):
    for piece, (array, k) in zip(piece_refs, terms):
        part = jnp.dot(piece[...], weight_refs[array][k], preferred_element_type=F32)
        total = part if total is None else total + part
    return total


def fold_kernel(r, terms, places, info_ref, *refs):
    out_ref, back_all, sems = refs[-3:]
    count = len(terms)
    pieces = refs[:count]
    slot = slot_of(r - (info_ref[1] - info_ref[0]), back_all.shape[0] - 1)
    copies = [pltpu.make_async_copy(pieces[i], back_all.at[slot, places[i]], sems.at[i]) for i in range(count)]
    for copy in copies:
        copy.start()
    out_ref[...] = fold_terms(None, pieces, refs[count : count + 2], terms)
    for copy in copies:
        copy.wait()


def fold(r, info, pieces, weights, terms, places, micro, stored):
    steps, rows = pieces[0].shape[0], weights[0].shape[2]
    args = (info, *pieces, *[in_vmem(w) for w in weights])
    n = len(args)
    return pl.pallas_call(
        lambda *refs: fold_kernel(r, terms, places, *refs),
        in_specs=[smem_spec()] + [vmem_spec()] * (n - 1) + [hbm_spec()] * len(stored),
        out_specs=[vmem_spec(), hbm_spec()],
        out_shape=[
            jax.ShapeDtypeStruct((steps, rows), F32),
            pltpu.HBM((micro + 1, 2 * weights[0].shape[0], *pieces[0].shape), BF16),
        ],
        input_output_aliases={n: 1} if stored else {},
        scratch_shapes=[pltpu.SemaphoreType.DMA((len(pieces),))],
        compiler_params=params(8),
        cost_estimate=cost(2 * pieces[0].size * rows * len(terms), 2 * rows * rows * len(terms)),
        name="fold",
    )(*args, *in_hbm(stored))


def back_kernel(r, terms, places, onward, info_ref, acc_ref, wd_ref, back_ref, weight_ref, *refs):
    piece_refs = refs[: len(terms)]
    deriv_all = refs[len(terms)]
    outs = refs[-7 if onward else -6 :]
    back_all, grad_all, padded, deriv_ref, grad_ref, sems = outs[-6:]
    taps, packs, pack, unused = wd_ref.shape
    steps, chans = acc_ref.shape
    half = taps // 2
    slot = slot_of(r - (info_ref[1] - info_ref[0]), deriv_all.shape[0] - 1)
    fetch = pltpu.make_async_copy(deriv_all.at[slot], deriv_ref, sems.at[0])
    fetch.start()
    copies = [
        pltpu.make_async_copy(piece_refs[i], back_all.at[slot, places[i]], sems.at[2 + i]) for i in range(len(terms))
    ]
    for copy in copies:
        copy.start()
    total = fold_terms(acc_ref[...], piece_refs, [weight_ref], terms)
    fetch.wait()
    grad = (total * deriv_ref[...]).astype(BF16)
    grad_ref[...] = grad
    put = pltpu.make_async_copy(grad_ref, grad_all.at[slot], sems.at[1])
    put.start()
    if onward:
        out_ref = outs[0]
        fill_padded(padded, grad.astype(F32))
        for p in range(packs):
            cols = slice(p * pack, (p + 1) * pack)
            out = back_ref[:, cols].astype(F32)
            for k in range(taps):
                start = PAD + half - k
                out = out + jnp.dot(
                    padded[start : start + steps, cols].astype(BF16), wd_ref[k, p], preferred_element_type=F32
                )
            out_ref[:, cols] = out.astype(BF16)
    put.wait()
    for copy in copies:
        copy.wait()


def conv_backward(r, info, acc, deriv_all, wd, back, weight, pieces, terms, places, onward, back_all, stored):
    steps, chans = acc.shape
    args = (info, acc, in_vmem(wd), back, in_vmem(weight), *pieces)
    n = len(args)
    outs = 1 if onward else 0
    return pl.pallas_call(
        lambda *refs: back_kernel(r, terms, places, onward, *refs),
        in_specs=[smem_spec()] + [vmem_spec()] * (n - 1) + [hbm_spec()] * (2 + len(stored)),
        out_specs=[vmem_spec()] * outs + [hbm_spec()] * 2,
        out_shape=[jax.ShapeDtypeStruct((steps, chans), BF16)] * outs
        + [pltpu.HBM(back_all.shape, BF16), pltpu.HBM((back_all.shape[0], steps, chans), BF16)],
        input_output_aliases={n + 1: outs, n + 2: outs + 1} if stored else {n + 1: outs},
        scratch_shapes=[
            pltpu.VMEM((steps + 2 * PAD, chans), F32),
            pltpu.VMEM((steps, chans), F32),
            pltpu.VMEM((steps, chans), BF16),
            pltpu.SemaphoreType.DMA((2 + len(pieces),)),
        ],
        compiler_params=params(8),
        cost_estimate=cost(2 * steps * chans * wd.shape[2] * wd.shape[0], 2 * wd.size),
        name="conv_backward",
    )(*args, *in_hbm([deriv_all, back_all, *stored]))


def grads_kernel(pack, place_ref, act_all, back_all, state_all, grad_all, point_ref, conv_ref, *scratch):
    acts, backs, outs, turned, states, grads, padded, turned_states, conv_out = scratch[:9]
    act_sems, in_sems, out_sems, conv_sem = scratch[9:]
    unused, count, steps, chans = back_all.shape
    micro = acts.shape[0]
    depth = backs.shape[0]
    bands = out_sems.shape[1]
    band = chans // bands
    taps, width = conv_out.shape[:2]
    half = taps // 2
    span = steps + 2 * PAD

    def fetch(j):
        return [
            pltpu.make_async_copy(
                back_all.at[m, j], backs.at[j % depth, pl.ds(m * steps, steps), :], in_sems.at[j % depth, m]
            )
            for m in range(micro)
        ]

    def put(j):
        start = pl.multiple_of(place_ref[j] * chans, 128)
        return [
            pltpu.make_async_copy(
                outs.at[j % depth, pl.ds(i * band, band), :],
                point_ref.at[0, pl.ds(i * band, band), pl.ds(start, chans)],
                out_sems.at[j % depth, i],
            )
            for i in range(bands)
        ]

    loads = [
        pltpu.make_async_copy(source.at[m], target.at[m], act_sems.at[i, m])
        for i, (source, target) in enumerate(((act_all, acts), (grad_all, grads), (state_all, states)))
        for m in range(micro)
    ]
    for copy in loads[:micro]:
        copy.start()
    for j in range(min(depth - 1, count)):
        for copy in fetch(j):
            copy.start()
    for copy in loads[micro:]:
        copy.start()

    def prepare():
        for copy in loads[micro:]:
            copy.wait()
        for m in range(micro):
            padded[m * span : m * span + PAD, :] = jnp.zeros((PAD, chans), F32)
            padded[m * span + PAD : m * span + PAD + steps, :] = grads[m].astype(F32)
            padded[m * span + PAD + steps : (m + 1) * span, :] = jnp.zeros((PAD, chans), F32)
            turned_states[:, m * steps : (m + 1) * steps] = states[m].astype(F32).T.astype(BF16)

    def conv_task(p, k):
        cols = slice(p * pack, (p + 1) * pack)
        start = PAD + half - k
        shifted = jnp.concatenate(
            [padded[m * span + start : m * span + start + steps, cols].astype(BF16) for m in range(micro)], axis=0
        )
        full = jnp.dot(turned_states[cols, :], shifted, preferred_element_type=F32)
        lane = lax.broadcasted_iota(jnp.int32, (width, pack), 1) // width
        out = jnp.zeros((width, pack), F32)
        for g in range(pack // width):
            out = jnp.where(lane == g, full[g * width : (g + 1) * width], out)
        conv_out[k, :, cols] = out

    tasks = [(p, k) for p in range(chans // pack) for k in range(taps)]
    each = -(-len(tasks) // max(1, count - 1))
    for m in range(micro):
        loads[m].wait()
        turned[:, m * steps : (m + 1) * steps] = acts[m].astype(F32).T.astype(BF16)
    for j in range(count):
        if j + depth - 1 < count:
            for copy in fetch(j + depth - 1):
                copy.start()
        for copy in fetch(j):
            copy.wait()
        if j >= depth:
            for copy in put(j - depth):
                copy.wait()
        outs[j % depth] = jnp.dot(turned[...], backs[j % depth], preferred_element_type=F32)
        for copy in put(j):
            copy.start()
        if j == 0:
            prepare()
        for p, k in tasks[j * each : (j + 1) * each]:
            conv_task(p, k)
    last_copy = pltpu.make_async_copy(conv_out, conv_ref.at[0], conv_sem)
    last_copy.start()
    for j in range(max(0, count - depth), count):
        for copy in put(j):
            copy.wait()
    last_copy.wait()


def grads(place, act_all, back_all, state_all, grad_all, micro, columns, taps, width, pack):
    unused, count, steps, chans = back_all.shape
    depth = 3
    bands = 4 if chans >= 256 else 1
    field = pltpu.VMEM((micro, steps, chans), BF16)
    return pl.pallas_call(
        lambda *refs: grads_kernel(pack, *refs),
        in_specs=[smem_spec()] + [hbm_spec()] * 4,
        out_specs=[hbm_spec()] * 2,
        out_shape=[pltpu.HBM((1, chans, columns), F32), pltpu.HBM((1, taps, width, chans), F32)],
        scratch_shapes=[
            field,
            pltpu.VMEM((depth, micro * steps, chans), BF16),
            pltpu.VMEM((depth, chans, chans), F32),
            pltpu.VMEM((chans, micro * steps), BF16),
            field,
            field,
            pltpu.VMEM((micro * (steps + 2 * PAD), chans), F32),
            pltpu.VMEM((chans, micro * steps), BF16),
            pltpu.VMEM((taps, width, chans), F32),
            pltpu.SemaphoreType.DMA((3, micro)),
            pltpu.SemaphoreType.DMA((depth, micro)),
            pltpu.SemaphoreType.DMA((depth, bands)),
            pltpu.SemaphoreType.DMA,
        ],
        compiler_params=params(32),
        cost_estimate=cost(2 * micro * steps * chans * columns, 4 * chans * columns + 2 * micro * steps * columns),
        name="grads",
    )(place, *in_hbm([act_all, back_all, state_all, grad_all]))


def local(inputs, labels, conv_weight, point_weight, head_weight):
    micro, steps, chans = inputs.shape
    unused, taps, width, unused_chans = conv_weight.shape
    pack = min(256, chans)
    section = lax.axis_index("section")
    n_section = lax.axis_size("section")
    last = n_section - 1
    n_chan = lax.axis_size("chan")
    chips = n_chan // 2
    chan = lax.axis_index("chan")
    chip, parity = chan // 2, chan % 2
    rounds = micro + n_section - 1

    def across(value, bits):
        return lax.ppermute(value, "chan", [(i, i ^ bits) for i in range(n_chan)])

    def along(value, step):
        pairs = [(i, i + step) for i in range(n_section) if 0 <= i + step < n_section]
        return lax.ppermute(value, "section", pairs)

    wd = block_diagonal(conv_weight[0], pack)
    weights = point_weight[0]
    place = jnp.stack([(chip ^ k) * 2 + (parity ^ p) for k in range(chips) for p in range(2)]).astype(jnp.int32)
    own, other = split(place, weights, chips)
    twin = load(across(other, 1))
    turned = {}
    head_rows = jnp.pad(head_weight.T, ((0, CROWS - CLASSES), (0, 0)))

    order = sorted(range(1, chips), key=lambda k: -bin(k).count("1"))
    info = jnp.stack([section, jnp.int32(last)]).astype(jnp.int32)
    zero = jnp.zeros((steps, chans), BF16)
    kept, gone = [], []
    tops = {}
    heads = jnp.stack([head_rows] + [across(head_rows, 2 * k) for k in range(1, chips)])

    def forward(r, recv):
        nonlocal kept
        state, act, deriv = conv_forward(info, inputs[min(r, micro - 1)], recv, wd)
        act_twin = across(act, 1)
        arrived, sent, score = {}, [], []
        head = [heads] if r >= last else []
        for k in order:
            out, *score = mix(act, act_twin, own, twin, k, *head, *score)
            sent.append(out)
            arrived[k] = across(out, 2 * k)
        mine, *rest = mix_own(r, info, act, act_twin, own, twin, state, deriv, kept, micro, *head, *score)
        kept = rest[-3:]
        if r >= last:
            score = rest[0] + across(rest[0], 1)
            score = score + sum(across(score, 2 * k) for k in range(1, chips))
            tops[r - last] = top_back(score, labels[r - last][None, :], head_rows, LOSS_SCALE / (micro * steps))

        def finish(after):
            return along(sum_state(mine, [arrived[k] for k in range(1, chips)], after), 1)

        return finish, sent + [mine]

    def backward(r, recv):
        nonlocal gone
        back = recv
        if r < micro:
            back = choose(info, tops[r], recv)
        pieces = {0: back}
        for k in order:
            pieces[k] = across(back, 2 * k)
        rest = list(range(1, chips))
        twins = {0: across(back, 1)}
        twins.update({k: across(pieces[k], 1) for k in rest})
        onward = r + 1 < rounds
        terms = [(1, 0)] + [(0, k) for k in range(chips)]
        places = [1] + [2 * k for k in range(chips)]
        listed = [twins[0]] + [pieces[k] for k in range(chips)]
        acc, back_all = fold(r, info, listed, [turned["own"], turned["other"]], terms, places, micro, gone[:1])
        terms, places = [(0, k) for k in rest], [2 * k + 1 for k in rest]
        listed = [twins[k] for k in rest]
        *back, back_all, grad_all = conv_backward(
            r, info, acc, kept[2], turned["wd"], back, turned["other"], listed, terms, places, onward, back_all, gone[1:]
        )
        gone = [back_all, grad_all]
        return along(back[0], -1) if onward else None

    ahead, behind = zero, zero
    for t in range(rounds + n_section):
        if t < rounds:
            finish, made = forward(t, ahead)
        after = []
        if t == 0:
            own_turned, own_mark = turn(own, made[-1:])
            other_turned, other_mark = turn(other, made[-1:])
            wd_turned, wd_mark = turn(wd.reshape(-1, pack, pack), made[-1:])
            turned.update(own=own_turned, other=other_turned, wd=wd_turned.reshape(wd.shape))
            after = [own_mark, other_mark, wd_mark]
        if t >= n_section:
            behind = backward(t - n_section, behind)
        if t + 1 < rounds:
            ahead = finish(after)

    grad_point, grad_conv = grads(
        place, kept[0], gone[0], kept[1], gone[1], micro, point_weight.shape[2], taps, width, pack
    )
    return grad_point, grad_conv


def solution(mesh):
    placed = (
        P(None, None, "chan"),
        P(),
        P("section", None, None, "chan"),
        P("section", "chan", None),
        P("chan", None),
    )
    return jax.shard_map(
        local,
        mesh=mesh,
        in_specs=placed,
        out_specs=(P("section", "chan", None), P("section", None, None, "chan")),
        check_vma=False,
    )
```

```python
import jax
import jax.numpy as jnp
from jax import lax
from jax.experimental import pallas as pl
from jax.experimental.pallas import tpu as pltpu
from jax.sharding import PartitionSpec as P

CLASSES = 3
LOSS_SCALE = 2048
CROWS = 8
PAD = 8
F32 = jnp.float32
BF16 = jnp.bfloat16
CUTS = 1
AHEAD_CUTS = 2
NT = (((1,), (1,)), ((), ()))
TN = (((0,), (0,)), ((), ()))


def params(mib):
    return pltpu.CompilerParams(vmem_limit_bytes=mib * 1024 * 1024)


def cost(flops, moved):
    return pl.CostEstimate(flops=int(flops), bytes_accessed=int(moved), transcendentals=0)


def vmem_spec():
    return pl.BlockSpec(memory_space=pltpu.VMEM)


def smem_spec():
    return pl.BlockSpec(memory_space=pltpu.SMEM)


def block_diagonal(kernel, pack):
    taps, width, chans = kernel.shape
    shaped = jnp.transpose(kernel.reshape(taps, width, chans // pack, pack), (0, 2, 1, 3))
    tiled = jnp.tile(shaped, (1, 1, pack // width, 1))
    row = jnp.arange(pack)[:, None] // width
    col = jnp.arange(pack)[None, :] // width
    return jnp.where(row == col, tiled, jnp.zeros_like(tiled))


def fill_padded(padded, field):
    steps, chans = field.shape
    padded[0:PAD, :] = jnp.zeros((PAD, chans), F32)
    padded[PAD : PAD + steps, :] = field
    padded[PAD + steps : PAD + steps + PAD, :] = jnp.zeros((PAD, chans), F32)


def slot_of(index, micro):
    return jnp.where((index >= 0) & (index < micro), index, micro)


def in_hbm(arrays):
    return [pltpu.with_memory_space_constraint(a, pltpu.HBM) for a in arrays]


def join(refs):
    return jnp.concatenate([ref[...] for ref in refs], axis=0)


def in_vmem(array):
    return pltpu.with_memory_space_constraint(array, pltpu.VMEM)


def hbm_spec():
    return pl.BlockSpec(memory_space=pltpu.HBM)


def split_kernel(side, place_ref, weights, out_ref, sems):
    chips, unused, chans = out_ref.shape
    copies = []
    for k in range(chips):
        start = pl.multiple_of(place_ref[2 * k + side] * chans, 128)
        copies.append(pltpu.make_async_copy(weights.at[:, pl.ds(start, chans)], out_ref.at[k], sems.at[k]))
    for copy in copies:
        copy.start()
    for copy in copies:
        copy.wait()


def split(place, weights, chips, side):
    rows = weights.shape[0]
    return pl.pallas_call(
        lambda *refs: split_kernel(side, *refs),
        in_specs=[smem_spec(), hbm_spec()],
        out_specs=vmem_spec(),
        out_shape=jax.ShapeDtypeStruct((chips, rows, rows), weights.dtype),
        scratch_shapes=[pltpu.SemaphoreType.DMA((chips,))],
        compiler_params=params(8),
        cost_estimate=cost(0, 2 * weights.size),
        name="split",
    )(place, *in_hbm([weights]))


def load_kernel(source, out_ref, sems):
    chips = out_ref.shape[0]
    copies = [pltpu.make_async_copy(source.at[k], out_ref.at[k], sems.at[k]) for k in range(chips)]
    for copy in copies:
        copy.start()
    for copy in copies:
        copy.wait()


def load(array):
    return pl.pallas_call(
        load_kernel,
        in_specs=[hbm_spec()],
        out_specs=vmem_spec(),
        out_shape=jax.ShapeDtypeStruct(array.shape, array.dtype),
        scratch_shapes=[pltpu.SemaphoreType.DMA((array.shape[0],))],
        compiler_params=params(8),
        cost_estimate=cost(0, 4 * array.size),
        name="load",
    )(*in_hbm([array]))


def turn_weights_kernel(source, *refs):
    out_ref, mark_ref = refs[-2:]
    mark_ref[...] = jnp.zeros_like(mark_ref)
    for k in range(out_ref.shape[0]):
        out_ref[k] = source[k].astype(F32).T.astype(BF16)


def turn(array, after):
    count, rows, columns = array.shape
    return pl.pallas_call(
        turn_weights_kernel,
        in_specs=[vmem_spec()] * (1 + len(after)),
        out_specs=[vmem_spec()] * 2,
        out_shape=[jax.ShapeDtypeStruct((count, columns, rows), BF16), jax.ShapeDtypeStruct((8, 128), F32)],
        compiler_params=params(8),
        cost_estimate=cost(0, 4 * array.size),
        name="turn",
    )(array, *after)


def conv_kernel(info_ref, fresh_ref, wd_ref, *refs):
    *recv_refs, state_ref, act_ref, deriv_ref, padded = refs
    taps, packs, pack, unused = wd_ref.shape
    steps, chans = fresh_ref.shape
    half = taps // 2
    state = jnp.where(info_ref[0] == 0, fresh_ref[...], join(recv_refs))
    state_ref[...] = state
    fill_padded(padded, state.astype(F32))
    for p in range(packs):
        cols = slice(p * pack, (p + 1) * pack)
        out = jnp.zeros((steps, pack), F32)
        for k in range(taps):
            start = PAD + k - half
            out = out + jnp.dot(
                padded[start : start + steps, cols].astype(BF16), wd_ref[k, p], preferred_element_type=F32
            )
        sig = jax.nn.sigmoid(out)
        act_ref[:, cols] = (out * sig).astype(BF16)
        deriv_ref[:, cols] = sig * (1.0 + out * (1.0 - sig))


def conv_forward(info, fresh, recv, wd):
    steps, chans = fresh.shape
    one = jax.ShapeDtypeStruct((steps, chans), BF16)
    return pl.pallas_call(
        conv_kernel,
        in_specs=[smem_spec()] + [vmem_spec()] * (2 + len(recv)),
        out_specs=[vmem_spec()] * 3,
        out_shape=[one, one, jax.ShapeDtypeStruct((steps, chans), F32)],
        scratch_shapes=[pltpu.VMEM((steps + 2 * PAD, chans), F32)],
        compiler_params=params(12),
        cost_estimate=cost(2 * steps * chans * wd.shape[2] * wd.shape[0], 2 * wd.size),
        name="conv_forward",
    )(info, fresh, in_vmem(wd), *recv)


def scored(head_ref, k, total, before_ref):
    high = total.astype(BF16)
    low = (total - high.astype(F32)).astype(BF16)
    score = lax.dot_general(head_ref[k], high, NT, preferred_element_type=F32)
    score = score + lax.dot_general(head_ref[k], low, NT, preferred_element_type=F32)
    return score if before_ref is None else score + before_ref[...]


def mix_kernel(k, cuts, head, before, a_ref, b_ref, wa_ref, wb_ref, *refs):
    total = jnp.dot(a_ref[...], wa_ref[k], preferred_element_type=F32)
    total = total + jnp.dot(b_ref[...], wb_ref[k], preferred_element_type=F32)
    sent = total.astype(BF16)
    outs = refs[-cuts:] if not head else refs[-cuts - 1 : -1]
    rows = outs[0].shape[0]
    for i in range(cuts):
        outs[i][...] = sent[i * rows : (i + 1) * rows]
    if not head:
        return
    score_ref = refs[-1]
    score_ref[...] = scored(refs[0], k, sent.astype(F32), refs[1] if before else None)


def mix(act, act_twin, wa, wb, k, cuts, heads=None, before=None):
    steps, chans = act.shape
    args = (act, act_twin, in_vmem(wa), in_vmem(wb)) + (() if heads is None else (heads,))
    args = args + (() if before is None else (before,))
    shapes = [jax.ShapeDtypeStruct((steps // cuts, wa.shape[2]), BF16)] * cuts
    if heads is not None:
        shapes.append(jax.ShapeDtypeStruct((CROWS, steps), F32))
    return pl.pallas_call(
        lambda *refs: mix_kernel(k, cuts, heads is not None, before is not None, *refs),
        in_specs=[vmem_spec()] * len(args),
        out_specs=[vmem_spec()] * len(shapes),
        out_shape=shapes,
        compiler_params=params(8),
        cost_estimate=cost(4 * steps * chans * wa.shape[2], 4 * wa[0].size),
        name="mix",
    )(*args)


def mix_own_kernel(r, head, info_ref, a_ref, b_ref, wa_ref, wb_ref, state_ref, deriv_ref, *refs):
    outs = refs[-6 if head else -5 :]
    act_all, state_all, deriv_all, sems = outs[-4:]
    k, slot = 0, slot_of(r - info_ref[0], act_all.shape[0] - 1)
    copies = [
        pltpu.make_async_copy(a_ref, act_all.at[slot], sems.at[0]),
        pltpu.make_async_copy(state_ref, state_all.at[slot], sems.at[1]),
        pltpu.make_async_copy(deriv_ref, deriv_all.at[slot], sems.at[2]),
    ]
    for copy in copies:
        copy.start()
    total = jnp.dot(a_ref[...], wa_ref[k], preferred_element_type=F32)
    total = total + jnp.dot(b_ref[...], wb_ref[k], preferred_element_type=F32)
    total = total + state_ref[...].astype(F32)
    outs[0][...] = total
    if head:
        outs[1][...] = scored(refs[0], k, total, refs[1])
    for copy in copies:
        copy.wait()


def mix_own(r, info, act, act_twin, wa, wb, state, deriv, stored, micro, heads=None, before=None):
    steps, chans = act.shape
    full = (micro + 1, steps, chans)
    args = (info, act, act_twin, in_vmem(wa), in_vmem(wb), state, deriv)
    args = args + (() if heads is None else (heads, before))
    n = len(args)
    shapes = [jax.ShapeDtypeStruct((steps, chans), F32)]
    if heads is not None:
        shapes.append(jax.ShapeDtypeStruct((CROWS, steps), F32))
    outs = len(shapes)
    return pl.pallas_call(
        lambda *refs: mix_own_kernel(r, heads is not None, *refs),
        in_specs=[smem_spec()] + [vmem_spec()] * (n - 1) + [hbm_spec()] * len(stored),
        out_specs=[vmem_spec()] * outs + [hbm_spec()] * 3,
        out_shape=shapes + [pltpu.HBM(full, BF16), pltpu.HBM(full, BF16), pltpu.HBM(full, F32)],
        input_output_aliases={n + i: outs + i for i in range(3)} if stored else {},
        scratch_shapes=[pltpu.SemaphoreType.DMA((3,))],
        compiler_params=params(8),
        cost_estimate=cost(4 * steps * chans * wa.shape[2], 4 * wa[0].size),
        name="mix_own",
    )(*args, *in_hbm(stored))


def sum_kernel(count, cut, own_ref, *refs):
    parts, out_ref = refs[:count], refs[-1]
    rows = out_ref.shape[0]
    total = own_ref[cut * rows : (cut + 1) * rows]
    for part in parts:
        total = total + part[...].astype(F32)
    out_ref[...] = total.astype(BF16)


def sum_state(own, parts, cut, cuts, after):
    steps, chans = own.shape
    return pl.pallas_call(
        lambda *refs: sum_kernel(len(parts), cut, *refs),
        in_specs=[vmem_spec()] * (1 + len(parts) + len(after)),
        out_specs=vmem_spec(),
        out_shape=jax.ShapeDtypeStruct((steps // cuts, chans), BF16),
        compiler_params=params(8),
        cost_estimate=cost(steps * chans * 8, 8 * steps * chans),
        name="sum_state",
    )(own, *parts, *after)


def hold_kernel(source, *refs):
    refs[-1][...] = source[...]


def hold(array, after):
    return pl.pallas_call(
        hold_kernel,
        in_specs=[vmem_spec()] * (1 + len(after)),
        out_specs=vmem_spec(),
        out_shape=jax.ShapeDtypeStruct(array.shape, array.dtype),
        compiler_params=params(8),
        cost_estimate=cost(0, 4 * array.size),
        name="hold",
    )(array, *after)


def top_kernel(scale, score_ref, label_ref, head_ref, out_ref):
    score = score_ref[...]
    row = lax.broadcasted_iota(jnp.int32, score.shape, 0)
    hot = (label_ref[...] == row).astype(F32)
    top = (jax.nn.sigmoid(score) - hot) * scale
    top = jnp.where(row < CLASSES, top, 0.0)
    out_ref[...] = lax.dot_general(
        top, head_ref[...].astype(F32), TN, preferred_element_type=F32, precision=lax.Precision.HIGHEST
    ).astype(BF16)


def top_back(score, label_row, head_rows, scale):
    return pl.pallas_call(
        lambda *refs: top_kernel(scale, *refs),
        in_specs=[vmem_spec()] * 3,
        out_specs=vmem_spec(),
        out_shape=jax.ShapeDtypeStruct((score.shape[1], head_rows.shape[1]), BF16),
        compiler_params=params(8),
        name="top_back",
    )(score, label_row, head_rows)


def choose_kernel(cut, info_ref, top_ref, recv_ref, out_ref):
    rows = out_ref.shape[0]
    out_ref[...] = jnp.where(info_ref[0] == info_ref[1], top_ref[cut * rows : (cut + 1) * rows], recv_ref[...])


def choose(info, top, recv, cut):
    return pl.pallas_call(
        lambda *refs: choose_kernel(cut, *refs),
        in_specs=[smem_spec()] + [vmem_spec()] * 2,
        out_specs=vmem_spec(),
        out_shape=jax.ShapeDtypeStruct(recv.shape, BF16),
        compiler_params=params(8),
        cost_estimate=cost(0, 4 * recv.size),
        name="choose",
    )(info, top, recv)


def fold_terms(total, piece_refs, weight_refs, terms):
    for i, (array, k) in enumerate(terms):
        part = jnp.dot(join(piece_refs[i * CUTS : (i + 1) * CUTS]), weight_refs[array][k], preferred_element_type=F32)
        total = part if total is None else total + part
    return total


def store_copies(pieces, places, back_all, slot, sems):
    rows = pieces[0].shape[0]
    return [
        pltpu.make_async_copy(
            piece, back_all.at[slot, places[i // CUTS], pl.ds(i % CUTS * rows, rows), :], sems.at[i]
        )
        for i, piece in enumerate(pieces)
    ]


def fold_kernel(r, terms, places, info_ref, *refs):
    out_ref, back_all, sems = refs[-3:]
    count = CUTS * len(terms)
    pieces = refs[:count]
    slot = slot_of(r - (info_ref[1] - info_ref[0]), back_all.shape[0] - 1)
    copies = store_copies(pieces, places, back_all, slot, sems)
    for copy in copies:
        copy.start()
    out_ref[...] = fold_terms(None, pieces, refs[count : count + 2], terms)
    for copy in copies:
        copy.wait()


def fold(r, info, pieces, weights, terms, places, micro, stored):
    rows, chans = pieces[0].shape
    steps, columns = CUTS * rows, weights[0].shape[2]
    args = (info, *pieces, *[in_vmem(w) for w in weights])
    n = len(args)
    return pl.pallas_call(
        lambda *refs: fold_kernel(r, terms, places, *refs),
        in_specs=[smem_spec()] + [vmem_spec()] * (n - 1) + [hbm_spec()] * len(stored),
        out_specs=[vmem_spec(), hbm_spec()],
        out_shape=[
            jax.ShapeDtypeStruct((steps, columns), F32),
            pltpu.HBM((micro + 1, 2 * weights[0].shape[0], steps, chans), BF16),
        ],
        input_output_aliases={n: 1} if stored else {},
        scratch_shapes=[pltpu.SemaphoreType.DMA((len(pieces),))],
        compiler_params=params(8),
        cost_estimate=cost(2 * steps * chans * columns * len(terms), 2 * chans * columns * len(terms)),
        name="fold",
    )(*args, *in_hbm(stored))


def back_kernel(r, terms, places, onward, info_ref, acc_ref, wd_ref, weight_ref, *refs):
    count = CUTS * len(terms)
    piece_refs = refs[:count]
    back_refs = refs[count : count + CUTS]
    deriv_all = refs[count + CUTS]
    outs = refs[-6 - CUTS if onward else -6 :]
    back_all, grad_all, padded, deriv_ref, grad_ref, sems = outs[-6:]
    taps, packs, pack, unused = wd_ref.shape
    steps, chans = acc_ref.shape
    half = taps // 2
    slot = slot_of(r - (info_ref[1] - info_ref[0]), deriv_all.shape[0] - 1)
    fetch = pltpu.make_async_copy(deriv_all.at[slot], deriv_ref, sems.at[0])
    fetch.start()
    copies = store_copies(piece_refs, places, back_all, slot, sems.at[pl.ds(2, count)])
    for copy in copies:
        copy.start()
    total = fold_terms(acc_ref[...], piece_refs, [weight_ref], terms)
    fetch.wait()
    grad = (total * deriv_ref[...]).astype(BF16)
    grad_ref[...] = grad
    put = pltpu.make_async_copy(grad_ref, grad_all.at[slot], sems.at[1])
    put.start()
    if onward:
        rows = steps // CUTS
        fill_padded(padded, grad.astype(F32))
        for p in range(packs):
            cols = slice(p * pack, (p + 1) * pack)
            out = jnp.concatenate([ref[:, cols] for ref in back_refs], axis=0).astype(F32)
            for k in range(taps):
                start = PAD + half - k
                out = out + jnp.dot(
                    padded[start : start + steps, cols].astype(BF16), wd_ref[k, p], preferred_element_type=F32
                )
            for i in range(CUTS):
                outs[i][:, cols] = out[i * rows : (i + 1) * rows].astype(BF16)
    put.wait()
    for copy in copies:
        copy.wait()


def conv_backward(r, info, acc, deriv_all, wd, back, weight, pieces, terms, places, onward, back_all, stored):
    steps, chans = acc.shape
    args = (info, acc, in_vmem(wd), in_vmem(weight), *pieces, *back)
    n = len(args)
    outs = CUTS if onward else 0
    return pl.pallas_call(
        lambda *refs: back_kernel(r, terms, places, onward, *refs),
        in_specs=[smem_spec()] + [vmem_spec()] * (n - 1) + [hbm_spec()] * (2 + len(stored)),
        out_specs=[vmem_spec()] * outs + [hbm_spec()] * 2,
        out_shape=[jax.ShapeDtypeStruct((steps // CUTS, chans), BF16)] * outs
        + [pltpu.HBM(back_all.shape, BF16), pltpu.HBM((back_all.shape[0], steps, chans), BF16)],
        input_output_aliases={n + 1: outs, n + 2: outs + 1} if stored else {n + 1: outs},
        scratch_shapes=[
            pltpu.VMEM((steps + 2 * PAD, chans), F32),
            pltpu.VMEM((steps, chans), F32),
            pltpu.VMEM((steps, chans), BF16),
            pltpu.SemaphoreType.DMA((2 + len(pieces),)),
        ],
        compiler_params=params(8),
        cost_estimate=cost(2 * steps * chans * wd.shape[2] * wd.shape[0], 2 * wd.size),
        name="conv_backward",
    )(*args, *in_hbm([deriv_all, back_all, *stored]))


def grads_kernel(pack, place_ref, act_all, back_all, state_all, grad_all, point_ref, conv_ref, *scratch):
    acts, backs, outs, turned, states, grads, padded, turned_states, conv_out = scratch[:9]
    act_sems, in_sems, out_sems, conv_sem = scratch[9:]
    unused, count, steps, chans = back_all.shape
    micro = acts.shape[0]
    depth = backs.shape[0]
    bands = out_sems.shape[1]
    band = chans // bands
    taps, width = conv_out.shape[:2]
    half = taps // 2
    span = steps + 2 * PAD

    def fetch(j):
        return [
            pltpu.make_async_copy(
                back_all.at[m, j], backs.at[j % depth, pl.ds(m * steps, steps), :], in_sems.at[j % depth, m]
            )
            for m in range(micro)
        ]

    def put(j):
        start = pl.multiple_of(place_ref[j] * chans, 128)
        return [
            pltpu.make_async_copy(
                outs.at[j % depth, pl.ds(i * band, band), :],
                point_ref.at[0, pl.ds(i * band, band), pl.ds(start, chans)],
                out_sems.at[j % depth, i],
            )
            for i in range(bands)
        ]

    loads = [
        pltpu.make_async_copy(source.at[m], target.at[m], act_sems.at[i, m])
        for i, (source, target) in enumerate(((act_all, acts), (grad_all, grads), (state_all, states)))
        for m in range(micro)
    ]
    for copy in loads[:micro]:
        copy.start()
    for j in range(min(depth - 1, count)):
        for copy in fetch(j):
            copy.start()
    for copy in loads[micro:]:
        copy.start()

    def prepare():
        for copy in loads[micro:]:
            copy.wait()
        for m in range(micro):
            padded[m * span : m * span + PAD, :] = jnp.zeros((PAD, chans), F32)
            padded[m * span + PAD : m * span + PAD + steps, :] = grads[m].astype(F32)
            padded[m * span + PAD + steps : (m + 1) * span, :] = jnp.zeros((PAD, chans), F32)
            turned_states[:, m * steps : (m + 1) * steps] = states[m].astype(F32).T.astype(BF16)

    def conv_task(p, k):
        cols = slice(p * pack, (p + 1) * pack)
        start = PAD + half - k
        shifted = jnp.concatenate(
            [padded[m * span + start : m * span + start + steps, cols].astype(BF16) for m in range(micro)], axis=0
        )
        full = jnp.dot(turned_states[cols, :], shifted, preferred_element_type=F32)
        lane = lax.broadcasted_iota(jnp.int32, (width, pack), 1) // width
        out = jnp.zeros((width, pack), F32)
        for g in range(pack // width):
            out = jnp.where(lane == g, full[g * width : (g + 1) * width], out)
        conv_out[k, :, cols] = out

    tasks = [(p, k) for p in range(chans // pack) for k in range(taps)]
    each = -(-len(tasks) // max(1, count - 1))
    for m in range(micro):
        loads[m].wait()
        turned[:, m * steps : (m + 1) * steps] = acts[m].astype(F32).T.astype(BF16)
    for j in range(count):
        if j + depth - 1 < count:
            for copy in fetch(j + depth - 1):
                copy.start()
        for copy in fetch(j):
            copy.wait()
        if j >= depth:
            for copy in put(j - depth):
                copy.wait()
        outs[j % depth] = jnp.dot(turned[...], backs[j % depth], preferred_element_type=F32)
        for copy in put(j):
            copy.start()
        if j == 0:
            prepare()
        for p, k in tasks[j * each : (j + 1) * each]:
            conv_task(p, k)
    last_copy = pltpu.make_async_copy(conv_out, conv_ref.at[0], conv_sem)
    last_copy.start()
    for j in range(max(0, count - depth), count):
        for copy in put(j):
            copy.wait()
    last_copy.wait()


def grads(place, act_all, back_all, state_all, grad_all, micro, columns, taps, width, pack):
    unused, count, steps, chans = back_all.shape
    depth = 3
    bands = 4 if chans >= 256 else 1
    field = pltpu.VMEM((micro, steps, chans), BF16)
    return pl.pallas_call(
        lambda *refs: grads_kernel(pack, *refs),
        in_specs=[smem_spec()] + [hbm_spec()] * 4,
        out_specs=[hbm_spec()] * 2,
        out_shape=[pltpu.HBM((1, chans, columns), F32), pltpu.HBM((1, taps, width, chans), F32)],
        scratch_shapes=[
            field,
            pltpu.VMEM((depth, micro * steps, chans), BF16),
            pltpu.VMEM((depth, chans, chans), F32),
            pltpu.VMEM((chans, micro * steps), BF16),
            field,
            field,
            pltpu.VMEM((micro * (steps + 2 * PAD), chans), F32),
            pltpu.VMEM((chans, micro * steps), BF16),
            pltpu.VMEM((taps, width, chans), F32),
            pltpu.SemaphoreType.DMA((3, micro)),
            pltpu.SemaphoreType.DMA((depth, micro)),
            pltpu.SemaphoreType.DMA((depth, bands)),
            pltpu.SemaphoreType.DMA,
        ],
        compiler_params=params(32),
        cost_estimate=cost(2 * micro * steps * chans * columns, 4 * chans * columns + 2 * micro * steps * columns),
        name="grads",
    )(place, *in_hbm([act_all, back_all, state_all, grad_all]))


def local(inputs, labels, conv_weight, point_weight, head_weight):
    micro, steps, chans = inputs.shape
    unused, taps, width, unused_chans = conv_weight.shape
    pack = min(256, chans)
    section = lax.axis_index("section")
    n_section = lax.axis_size("section")
    last = n_section - 1
    n_chan = lax.axis_size("chan")
    chips = n_chan // 2
    chan = lax.axis_index("chan")
    chip, parity = chan // 2, chan % 2
    rounds = micro + n_section - 1

    def across(value, bits):
        return lax.ppermute(value, "chan", [(i, i ^ bits) for i in range(n_chan)])

    def along(value, step):
        pairs = [(i, i + step) for i in range(n_section) if 0 <= i + step < n_section]
        return lax.ppermute(value, "section", pairs)

    wd = block_diagonal(conv_weight[0], pack)
    weights = point_weight[0]
    place = jnp.stack([(chip ^ k) * 2 + (parity ^ p) for k in range(chips) for p in range(2)]).astype(jnp.int32)
    other = split(place, weights, chips, 1)
    own = split(place, weights, chips, 0)
    twin = load(across(other, 1))
    turned = {}
    head_rows = jnp.pad(head_weight.T, ((0, CROWS - CLASSES), (0, 0)))

    order = sorted(range(1, chips), key=lambda k: -bin(k).count("1"))
    info = jnp.stack([section, jnp.int32(last)]).astype(jnp.int32)
    zero = [jnp.zeros((steps // CUTS, chans), BF16)] * CUTS
    kept, gone = [], []
    tops = {}
    heads = None

    def forward(r, recv):
        nonlocal kept
        cuts = AHEAD_CUTS if r < n_section - 1 else 1
        state, act, deriv = conv_forward(info, inputs[min(r, micro - 1)], recv, wd)
        act_twin = across(act, 1)
        arrived, sent, score = {}, [], []
        head = [heads] if r >= last else []
        for k in order:
            out = mix(act, act_twin, own, twin, k, cuts, *head, *score)
            score = list(out[cuts:])
            sent.append(out[0])
            arrived[k] = [across(cut, 2 * k) for cut in out[:cuts]]
        mine, *rest = mix_own(r, info, act, act_twin, own, twin, state, deriv, kept, micro, *head, *score)
        kept = rest[-3:]
        if r >= last:
            score = rest[0] + across(rest[0], 1)
            score = score + sum(across(score, 2 * k) for k in range(1, chips))
            tops[r - last] = top_back(score, labels[r - last][None, :], head_rows, LOSS_SCALE / (micro * steps))

        def finish(after):
            parts = [[arrived[k][i] for k in range(1, chips)] for i in range(cuts)]
            return [along(sum_state(mine, parts[i], i, cuts, after), 1) for i in range(cuts)]

        return finish, sent + [mine]

    def backward(r, recv):
        nonlocal gone
        back = recv
        if r < micro:
            back = [choose(info, tops[r], recv[i], i) for i in range(CUTS)]
        pieces = {0: back}
        for k in order:
            pieces[k] = [None] * CUTS
        for i in range(CUTS):
            for k in order:
                pieces[k][i] = across(back[i], 2 * k)
        rest = list(range(1, chips))
        twins = {k: [across(cut, 1) for cut in pieces[k]] for k in range(chips)}
        onward = r + 1 < rounds
        terms = [(1, 0)] + [(0, k) for k in range(chips)]
        places = [1] + [2 * k for k in range(chips)]
        listed = twins[0] + [cut for k in range(chips) for cut in pieces[k]]
        acc, back_all = fold(r, info, listed, [turned["own"], turned["other"]], terms, places, micro, gone[:1])
        terms, places = [(0, k) for k in rest], [2 * k + 1 for k in rest]
        listed = [cut for k in rest for cut in twins[k]]
        *back, back_all, grad_all = conv_backward(
            r, info, acc, kept[2], turned["wd"], back, turned["other"], listed, terms, places, onward, back_all, gone[1:]
        )
        gone = [back_all, grad_all]
        return [along(cut, -1) for cut in back] if onward else None

    ahead, behind = zero, zero
    for t in range(rounds + n_section):
        if t < rounds:
            finish, made = forward(t, ahead)
        after = []
        if t == 0:
            own_turned, own_mark = turn(own, made[-1:])
            other_turned, other_mark = turn(other, made[-1:])
            wd_turned, wd_mark = turn(wd.reshape(-1, pack, pack), made[-1:])
            turned.update(own=own_turned, other=other_turned, wd=wd_turned.reshape(wd.shape))
            after = [own_mark, other_mark, wd_mark]
        if t == 1:
            held = hold(head_rows, made)
            heads = jnp.stack([held] + [across(held, 2 * k) for k in range(1, chips)])
            after = [heads]
        if t >= n_section:
            behind = backward(t - n_section, behind)
        if t + 1 < rounds:
            ahead = finish(after)

    grad_point, grad_conv = grads(
        place, kept[0], gone[0], kept[1], gone[1], micro, point_weight.shape[2], taps, width, pack
    )
    return grad_point, grad_conv


def solution(mesh):
    placed = (
        P(None, None, "chan"),
        P(),
        P("section", None, None, "chan"),
        P("section", "chan", None),
        P("chan", None),
    )
    return jax.shard_map(
        local,
        mesh=mesh,
        in_specs=placed,
        out_specs=(P("section", "chan", None), P("section", None, None, "chan")),
        check_vma=False,
    )
```

```python
import jax
import jax.numpy as jnp
from jax import lax
from jax.experimental import pallas as pl
from jax.experimental.pallas import tpu as pltpu
from jax.sharding import PartitionSpec as P

CLASSES = 3
LOSS_SCALE = 2048
CROWS = 8
PAD = 8
F32 = jnp.float32
BF16 = jnp.bfloat16
CUTS = 1
AHEAD_CUTS = 2
NT = (((1,), (1,)), ((), ()))
TN = (((0,), (0,)), ((), ()))


def params(mib):
    return pltpu.CompilerParams(vmem_limit_bytes=mib * 1024 * 1024)


def cost(flops, moved):
    return pl.CostEstimate(flops=int(flops), bytes_accessed=int(moved), transcendentals=0)


def vmem_spec():
    return pl.BlockSpec(memory_space=pltpu.VMEM)


def smem_spec():
    return pl.BlockSpec(memory_space=pltpu.SMEM)


def block_diagonal(kernel, pack):
    taps, width, chans = kernel.shape
    shaped = jnp.transpose(kernel.reshape(taps, width, chans // pack, pack), (0, 2, 1, 3))
    tiled = jnp.tile(shaped, (1, 1, pack // width, 1))
    row = jnp.arange(pack)[:, None] // width
    col = jnp.arange(pack)[None, :] // width
    return jnp.where(row == col, tiled, jnp.zeros_like(tiled))


def fill_padded(padded, field):
    steps, chans = field.shape
    padded[0:PAD, :] = jnp.zeros((PAD, chans), F32)
    padded[PAD : PAD + steps, :] = field
    padded[PAD + steps : PAD + steps + PAD, :] = jnp.zeros((PAD, chans), F32)


def slot_of(index, micro):
    return jnp.where((index >= 0) & (index < micro), index, micro)


def in_hbm(arrays):
    return [pltpu.with_memory_space_constraint(a, pltpu.HBM) for a in arrays]


def join(refs):
    return jnp.concatenate([ref[...] for ref in refs], axis=0)


def in_vmem(array):
    return pltpu.with_memory_space_constraint(array, pltpu.VMEM)


def hbm_spec():
    return pl.BlockSpec(memory_space=pltpu.HBM)


def split_kernel(side, place_ref, weights, out_ref, sems):
    chips, unused, chans = out_ref.shape
    copies = []
    for k in range(chips):
        start = pl.multiple_of(place_ref[2 * k + side] * chans, 128)
        copies.append(pltpu.make_async_copy(weights.at[:, pl.ds(start, chans)], out_ref.at[k], sems.at[k]))
    for copy in copies:
        copy.start()
    for copy in copies:
        copy.wait()


def split(place, weights, chips, side):
    rows = weights.shape[0]
    return pl.pallas_call(
        lambda *refs: split_kernel(side, *refs),
        in_specs=[smem_spec(), hbm_spec()],
        out_specs=vmem_spec(),
        out_shape=jax.ShapeDtypeStruct((chips, rows, rows), weights.dtype),
        scratch_shapes=[pltpu.SemaphoreType.DMA((chips,))],
        compiler_params=params(8),
        cost_estimate=cost(0, 2 * weights.size),
        name="split",
    )(place, *in_hbm([weights]))


def load_kernel(source, out_ref, sems):
    chips = out_ref.shape[0]
    copies = [pltpu.make_async_copy(source.at[k], out_ref.at[k], sems.at[k]) for k in range(chips)]
    for copy in copies:
        copy.start()
    for copy in copies:
        copy.wait()


def load(array):
    return pl.pallas_call(
        load_kernel,
        in_specs=[hbm_spec()],
        out_specs=vmem_spec(),
        out_shape=jax.ShapeDtypeStruct(array.shape, array.dtype),
        scratch_shapes=[pltpu.SemaphoreType.DMA((array.shape[0],))],
        compiler_params=params(8),
        cost_estimate=cost(0, 4 * array.size),
        name="load",
    )(*in_hbm([array]))


def turn_weights_kernel(source, *refs):
    out_ref, mark_ref = refs[-2:]
    mark_ref[...] = jnp.zeros_like(mark_ref)
    for k in range(out_ref.shape[0]):
        out_ref[k] = source[k].astype(F32).T.astype(BF16)


def turn(array, after):
    count, rows, columns = array.shape
    return pl.pallas_call(
        turn_weights_kernel,
        in_specs=[vmem_spec()] * (1 + len(after)),
        out_specs=[vmem_spec()] * 2,
        out_shape=[jax.ShapeDtypeStruct((count, columns, rows), BF16), jax.ShapeDtypeStruct((8, 128), F32)],
        compiler_params=params(8),
        cost_estimate=cost(0, 4 * array.size),
        name="turn",
    )(array, *after)


def conv_kernel(info_ref, fresh_ref, wd_ref, *refs):
    *recv_refs, state_ref, act_ref, deriv_ref, padded = refs
    taps, packs, pack, unused = wd_ref.shape
    steps, chans = fresh_ref.shape
    half = taps // 2
    state = jnp.where(info_ref[0] == 0, fresh_ref[...], join(recv_refs))
    state_ref[...] = state
    fill_padded(padded, state.astype(F32))
    for p in range(packs):
        cols = slice(p * pack, (p + 1) * pack)
        out = jnp.zeros((steps, pack), F32)
        for k in range(taps):
            start = PAD + k - half
            out = out + jnp.dot(
                padded[start : start + steps, cols].astype(BF16), wd_ref[k, p], preferred_element_type=F32
            )
        sig = jax.nn.sigmoid(out)
        act_ref[:, cols] = (out * sig).astype(BF16)
        deriv_ref[:, cols] = sig * (1.0 + out * (1.0 - sig))


def conv_forward(info, fresh, recv, wd):
    steps, chans = fresh.shape
    one = jax.ShapeDtypeStruct((steps, chans), BF16)
    return pl.pallas_call(
        conv_kernel,
        in_specs=[smem_spec()] + [vmem_spec()] * (2 + len(recv)),
        out_specs=[vmem_spec()] * 3,
        out_shape=[one, one, jax.ShapeDtypeStruct((steps, chans), F32)],
        scratch_shapes=[pltpu.VMEM((steps + 2 * PAD, chans), F32)],
        compiler_params=params(12),
        cost_estimate=cost(2 * steps * chans * wd.shape[2] * wd.shape[0], 2 * wd.size),
        name="conv_forward",
    )(info, fresh, in_vmem(wd), *recv)


def scored(head_ref, k, total, before_ref):
    high = total.astype(BF16)
    low = (total - high.astype(F32)).astype(BF16)
    score = lax.dot_general(head_ref[k], high, NT, preferred_element_type=F32)
    score = score + lax.dot_general(head_ref[k], low, NT, preferred_element_type=F32)
    return score if before_ref is None else score + before_ref[...]


def mix_kernel(k, cuts, head, before, a_ref, b_ref, wa_ref, wb_ref, *refs):
    total = jnp.dot(a_ref[...], wa_ref[k], preferred_element_type=F32)
    total = total + jnp.dot(b_ref[...], wb_ref[k], preferred_element_type=F32)
    sent = total.astype(BF16)
    outs = refs[-cuts:] if not head else refs[-cuts - 1 : -1]
    rows = outs[0].shape[0]
    for i in range(cuts):
        outs[i][...] = sent[i * rows : (i + 1) * rows]
    if not head:
        return
    score_ref = refs[-1]
    score_ref[...] = scored(refs[0], k, sent.astype(F32), refs[1] if before else None)


def mix(act, act_twin, wa, wb, k, cuts, heads=None, before=None):
    steps, chans = act.shape
    args = (act, act_twin, in_vmem(wa), in_vmem(wb)) + (() if heads is None else (heads,))
    args = args + (() if before is None else (before,))
    shapes = [jax.ShapeDtypeStruct((steps // cuts, wa.shape[2]), BF16)] * cuts
    if heads is not None:
        shapes.append(jax.ShapeDtypeStruct((CROWS, steps), F32))
    return pl.pallas_call(
        lambda *refs: mix_kernel(k, cuts, heads is not None, before is not None, *refs),
        in_specs=[vmem_spec()] * len(args),
        out_specs=[vmem_spec()] * len(shapes),
        out_shape=shapes,
        compiler_params=params(8),
        cost_estimate=cost(4 * steps * chans * wa.shape[2], 4 * wa[0].size),
        name="mix",
    )(*args)


def mix_own_kernel(r, head, info_ref, a_ref, b_ref, wa_ref, wb_ref, state_ref, deriv_ref, *refs):
    outs = refs[-6 if head else -5 :]
    act_all, state_all, deriv_all, sems = outs[-4:]
    k, slot = 0, slot_of(r - info_ref[0], act_all.shape[0] - 1)
    copies = [
        pltpu.make_async_copy(a_ref, act_all.at[slot], sems.at[0]),
        pltpu.make_async_copy(state_ref, state_all.at[slot], sems.at[1]),
        pltpu.make_async_copy(deriv_ref, deriv_all.at[slot], sems.at[2]),
    ]
    for copy in copies:
        copy.start()
    total = jnp.dot(a_ref[...], wa_ref[k], preferred_element_type=F32)
    total = total + jnp.dot(b_ref[...], wb_ref[k], preferred_element_type=F32)
    total = total + state_ref[...].astype(F32)
    outs[0][...] = total
    if head:
        outs[1][...] = scored(refs[0], k, total, refs[1])
    for copy in copies:
        copy.wait()


def mix_own(r, info, act, act_twin, wa, wb, state, deriv, stored, micro, heads=None, before=None):
    steps, chans = act.shape
    full = (micro + 1, steps, chans)
    args = (info, act, act_twin, in_vmem(wa), in_vmem(wb), state, deriv)
    args = args + (() if heads is None else (heads, before))
    n = len(args)
    shapes = [jax.ShapeDtypeStruct((steps, chans), F32)]
    if heads is not None:
        shapes.append(jax.ShapeDtypeStruct((CROWS, steps), F32))
    outs = len(shapes)
    return pl.pallas_call(
        lambda *refs: mix_own_kernel(r, heads is not None, *refs),
        in_specs=[smem_spec()] + [vmem_spec()] * (n - 1) + [hbm_spec()] * len(stored),
        out_specs=[vmem_spec()] * outs + [hbm_spec()] * 3,
        out_shape=shapes + [pltpu.HBM(full, BF16), pltpu.HBM(full, BF16), pltpu.HBM(full, F32)],
        input_output_aliases={n + i: outs + i for i in range(3)} if stored else {},
        scratch_shapes=[pltpu.SemaphoreType.DMA((3,))],
        compiler_params=params(8),
        cost_estimate=cost(4 * steps * chans * wa.shape[2], 4 * wa[0].size),
        name="mix_own",
    )(*args, *in_hbm(stored))


def sum_kernel(count, cut, own_ref, *refs):
    parts, out_ref = refs[:count], refs[-1]
    rows = out_ref.shape[0]
    total = own_ref[cut * rows : (cut + 1) * rows]
    for part in parts:
        total = total + part[...].astype(F32)
    out_ref[...] = total.astype(BF16)


def sum_state(own, parts, cut, cuts, after):
    steps, chans = own.shape
    return pl.pallas_call(
        lambda *refs: sum_kernel(len(parts), cut, *refs),
        in_specs=[vmem_spec()] * (1 + len(parts) + len(after)),
        out_specs=vmem_spec(),
        out_shape=jax.ShapeDtypeStruct((steps // cuts, chans), BF16),
        compiler_params=params(8),
        cost_estimate=cost(steps * chans * 8, 8 * steps * chans),
        name="sum_state",
    )(own, *parts, *after)


def hold_kernel(source, *refs):
    refs[-1][...] = source[...]


def hold(array, after):
    return pl.pallas_call(
        hold_kernel,
        in_specs=[vmem_spec()] * (1 + len(after)),
        out_specs=vmem_spec(),
        out_shape=jax.ShapeDtypeStruct(array.shape, array.dtype),
        compiler_params=params(8),
        cost_estimate=cost(0, 4 * array.size),
        name="hold",
    )(array, *after)


def top_kernel(scale, score_ref, label_ref, head_ref, out_ref):
    score = score_ref[...]
    row = lax.broadcasted_iota(jnp.int32, score.shape, 0)
    hot = (label_ref[...] == row).astype(F32)
    top = (jax.nn.sigmoid(score) - hot) * scale
    top = jnp.where(row < CLASSES, top, 0.0)
    out_ref[...] = lax.dot_general(
        top, head_ref[...].astype(F32), TN, preferred_element_type=F32, precision=lax.Precision.HIGHEST
    ).astype(BF16)


def top_back(score, label_row, head_rows, scale):
    return pl.pallas_call(
        lambda *refs: top_kernel(scale, *refs),
        in_specs=[vmem_spec()] * 3,
        out_specs=vmem_spec(),
        out_shape=jax.ShapeDtypeStruct((score.shape[1], head_rows.shape[1]), BF16),
        compiler_params=params(8),
        name="top_back",
    )(score, label_row, head_rows)


def choose_kernel(cut, info_ref, top_ref, recv_ref, out_ref):
    rows = out_ref.shape[0]
    out_ref[...] = jnp.where(info_ref[0] == info_ref[1], top_ref[cut * rows : (cut + 1) * rows], recv_ref[...])


def choose(info, top, recv, cut):
    return pl.pallas_call(
        lambda *refs: choose_kernel(cut, *refs),
        in_specs=[smem_spec()] + [vmem_spec()] * 2,
        out_specs=vmem_spec(),
        out_shape=jax.ShapeDtypeStruct(recv.shape, BF16),
        compiler_params=params(8),
        cost_estimate=cost(0, 4 * recv.size),
        name="choose",
    )(info, top, recv)


def fold_terms(total, piece_refs, weight_refs, terms):
    for i, (array, k) in enumerate(terms):
        part = jnp.dot(join(piece_refs[i * CUTS : (i + 1) * CUTS]), weight_refs[array][k], preferred_element_type=F32)
        total = part if total is None else total + part
    return total


def store_copies(pieces, places, back_all, slot, sems):
    rows = pieces[0].shape[0]
    return [
        pltpu.make_async_copy(
            piece, back_all.at[slot, places[i // CUTS], pl.ds(i % CUTS * rows, rows), :], sems.at[i]
        )
        for i, piece in enumerate(pieces)
    ]


def fold_kernel(r, terms, places, info_ref, *refs):
    out_ref, back_all, sems = refs[-3:]
    count = CUTS * len(terms)
    pieces = refs[:count]
    slot = slot_of(r - (info_ref[1] - info_ref[0]), back_all.shape[0] - 1)
    copies = store_copies(pieces, places, back_all, slot, sems)
    for copy in copies:
        copy.start()
    out_ref[...] = fold_terms(None, pieces, refs[count : count + 2], terms)
    for copy in copies:
        copy.wait()


def fold(r, info, pieces, weights, terms, places, micro, stored):
    rows, chans = pieces[0].shape
    steps, columns = CUTS * rows, weights[0].shape[2]
    args = (info, *pieces, *[in_vmem(w) for w in weights])
    n = len(args)
    return pl.pallas_call(
        lambda *refs: fold_kernel(r, terms, places, *refs),
        in_specs=[smem_spec()] + [vmem_spec()] * (n - 1) + [hbm_spec()] * len(stored),
        out_specs=[vmem_spec(), hbm_spec()],
        out_shape=[
            jax.ShapeDtypeStruct((steps, columns), F32),
            pltpu.HBM((micro + 1, 2 * weights[0].shape[0], steps, chans), BF16),
        ],
        input_output_aliases={n: 1} if stored else {},
        scratch_shapes=[pltpu.SemaphoreType.DMA((len(pieces),))],
        compiler_params=params(8),
        cost_estimate=cost(2 * steps * chans * columns * len(terms), 2 * chans * columns * len(terms)),
        name="fold",
    )(*args, *in_hbm(stored))


def back_kernel(r, terms, places, onward, info_ref, acc_ref, wd_ref, weight_ref, *refs):
    count = CUTS * len(terms)
    piece_refs = refs[:count]
    back_refs = refs[count : count + CUTS]
    deriv_all = refs[count + CUTS]
    outs = refs[-6 - CUTS if onward else -6 :]
    back_all, grad_all, padded, deriv_ref, grad_ref, sems = outs[-6:]
    taps, packs, pack, unused = wd_ref.shape
    steps, chans = acc_ref.shape
    half = taps // 2
    slot = slot_of(r - (info_ref[1] - info_ref[0]), deriv_all.shape[0] - 1)
    fetch = pltpu.make_async_copy(deriv_all.at[slot], deriv_ref, sems.at[0])
    fetch.start()
    copies = store_copies(piece_refs, places, back_all, slot, sems.at[pl.ds(2, count)])
    for copy in copies:
        copy.start()
    total = fold_terms(acc_ref[...], piece_refs, [weight_ref], terms)
    fetch.wait()
    grad = (total * deriv_ref[...]).astype(BF16)
    grad_ref[...] = grad
    put = pltpu.make_async_copy(grad_ref, grad_all.at[slot], sems.at[1])
    put.start()
    if onward:
        rows = steps // CUTS
        fill_padded(padded, grad.astype(F32))
        for p in range(packs):
            cols = slice(p * pack, (p + 1) * pack)
            out = jnp.concatenate([ref[:, cols] for ref in back_refs], axis=0).astype(F32)
            for k in range(taps):
                start = PAD + half - k
                out = out + jnp.dot(
                    padded[start : start + steps, cols].astype(BF16), wd_ref[k, p], preferred_element_type=F32
                )
            for i in range(CUTS):
                outs[i][:, cols] = out[i * rows : (i + 1) * rows].astype(BF16)
    put.wait()
    for copy in copies:
        copy.wait()


def conv_backward(r, info, acc, deriv_all, wd, back, weight, pieces, terms, places, onward, back_all, stored):
    steps, chans = acc.shape
    args = (info, acc, in_vmem(wd), in_vmem(weight), *pieces, *back)
    n = len(args)
    outs = CUTS if onward else 0
    return pl.pallas_call(
        lambda *refs: back_kernel(r, terms, places, onward, *refs),
        in_specs=[smem_spec()] + [vmem_spec()] * (n - 1) + [hbm_spec()] * (2 + len(stored)),
        out_specs=[vmem_spec()] * outs + [hbm_spec()] * 2,
        out_shape=[jax.ShapeDtypeStruct((steps // CUTS, chans), BF16)] * outs
        + [pltpu.HBM(back_all.shape, BF16), pltpu.HBM((back_all.shape[0], steps, chans), BF16)],
        input_output_aliases={n + 1: outs, n + 2: outs + 1} if stored else {n + 1: outs},
        scratch_shapes=[
            pltpu.VMEM((steps + 2 * PAD, chans), F32),
            pltpu.VMEM((steps, chans), F32),
            pltpu.VMEM((steps, chans), BF16),
            pltpu.SemaphoreType.DMA((2 + len(pieces),)),
        ],
        compiler_params=params(8),
        cost_estimate=cost(2 * steps * chans * wd.shape[2] * wd.shape[0], 2 * wd.size),
        name="conv_backward",
    )(*args, *in_hbm([deriv_all, back_all, *stored]))


def grads_kernel(pack, place_ref, act_all, back_all, state_all, grad_all, point_ref, conv_ref, *scratch):
    acts, backs, outs, turned, states, grads, padded, turned_states, conv_out = scratch[:9]
    act_sems, in_sems, out_sems, conv_sem = scratch[9:]
    unused, count, steps, chans = back_all.shape
    micro = acts.shape[0]
    depth = backs.shape[0]
    bands = out_sems.shape[1]
    band = chans // bands
    taps, width = conv_out.shape[:2]
    half = taps // 2
    span = steps + 2 * PAD

    def fetch(j):
        return [
            pltpu.make_async_copy(
                back_all.at[m, j], backs.at[j % depth, pl.ds(m * steps, steps), :], in_sems.at[j % depth, m]
            )
            for m in range(micro)
        ]

    def put(j):
        start = pl.multiple_of(place_ref[j] * chans, 128)
        return [
            pltpu.make_async_copy(
                outs.at[j % depth, pl.ds(i * band, band), :],
                point_ref.at[0, pl.ds(i * band, band), pl.ds(start, chans)],
                out_sems.at[j % depth, i],
            )
            for i in range(bands)
        ]

    loads = [
        pltpu.make_async_copy(source.at[m], target.at[m], act_sems.at[i, m])
        for i, (source, target) in enumerate(((act_all, acts), (grad_all, grads), (state_all, states)))
        for m in range(micro)
    ]
    for copy in loads[:micro]:
        copy.start()
    for j in range(min(depth - 1, count)):
        for copy in fetch(j):
            copy.start()
    for copy in loads[micro:]:
        copy.start()

    def prepare():
        for copy in loads[micro:]:
            copy.wait()
        for m in range(micro):
            padded[m * span : m * span + PAD, :] = jnp.zeros((PAD, chans), F32)
            padded[m * span + PAD : m * span + PAD + steps, :] = grads[m].astype(F32)
            padded[m * span + PAD + steps : (m + 1) * span, :] = jnp.zeros((PAD, chans), F32)
            turned_states[:, m * steps : (m + 1) * steps] = states[m].astype(F32).T.astype(BF16)

    def conv_task(p, k):
        cols = slice(p * pack, (p + 1) * pack)
        start = PAD + half - k
        shifted = jnp.concatenate(
            [padded[m * span + start : m * span + start + steps, cols].astype(BF16) for m in range(micro)], axis=0
        )
        full = jnp.dot(turned_states[cols, :], shifted, preferred_element_type=F32)
        lane = lax.broadcasted_iota(jnp.int32, (width, pack), 1) // width
        out = jnp.zeros((width, pack), F32)
        for g in range(pack // width):
            out = jnp.where(lane == g, full[g * width : (g + 1) * width], out)
        conv_out[k, :, cols] = out

    tasks = [(p, k) for p in range(chans // pack) for k in range(taps)]
    each = -(-len(tasks) // max(1, count - 1))
    for m in range(micro):
        loads[m].wait()
        turned[:, m * steps : (m + 1) * steps] = acts[m].astype(F32).T.astype(BF16)
    for j in range(count):
        if j + depth - 1 < count:
            for copy in fetch(j + depth - 1):
                copy.start()
        for copy in fetch(j):
            copy.wait()
        if j >= depth:
            for copy in put(j - depth):
                copy.wait()
        outs[j % depth] = jnp.dot(turned[...], backs[j % depth], preferred_element_type=F32)
        for copy in put(j):
            copy.start()
        if j == 0:
            prepare()
        for p, k in tasks[j * each : (j + 1) * each]:
            conv_task(p, k)
    last_copy = pltpu.make_async_copy(conv_out, conv_ref.at[0], conv_sem)
    last_copy.start()
    for j in range(max(0, count - depth), count):
        for copy in put(j):
            copy.wait()
    last_copy.wait()


def grads(place, act_all, back_all, state_all, grad_all, micro, columns, taps, width, pack):
    unused, count, steps, chans = back_all.shape
    depth = 3
    bands = 4 if chans >= 256 else 1
    field = pltpu.VMEM((micro, steps, chans), BF16)
    return pl.pallas_call(
        lambda *refs: grads_kernel(pack, *refs),
        in_specs=[smem_spec()] + [hbm_spec()] * 4,
        out_specs=[hbm_spec()] * 2,
        out_shape=[pltpu.HBM((1, chans, columns), F32), pltpu.HBM((1, taps, width, chans), F32)],
        scratch_shapes=[
            field,
            pltpu.VMEM((depth, micro * steps, chans), BF16),
            pltpu.VMEM((depth, chans, chans), F32),
            pltpu.VMEM((chans, micro * steps), BF16),
            field,
            field,
            pltpu.VMEM((micro * (steps + 2 * PAD), chans), F32),
            pltpu.VMEM((chans, micro * steps), BF16),
            pltpu.VMEM((taps, width, chans), F32),
            pltpu.SemaphoreType.DMA((3, micro)),
            pltpu.SemaphoreType.DMA((depth, micro)),
            pltpu.SemaphoreType.DMA((depth, bands)),
            pltpu.SemaphoreType.DMA,
        ],
        compiler_params=params(32),
        cost_estimate=cost(2 * micro * steps * chans * columns, 4 * chans * columns + 2 * micro * steps * columns),
        name="grads",
    )(place, *in_hbm([act_all, back_all, state_all, grad_all]))


def local(inputs, labels, conv_weight, point_weight, head_weight):
    micro, steps, chans = inputs.shape
    unused, taps, width, unused_chans = conv_weight.shape
    pack = min(256, chans)
    section = lax.axis_index("section")
    n_section = lax.axis_size("section")
    last = n_section - 1
    n_chan = lax.axis_size("chan")
    chips = n_chan // 2
    chan = lax.axis_index("chan")
    chip, parity = chan // 2, chan % 2
    rounds = micro + n_section - 1

    def across(value, bits):
        return lax.ppermute(value, "chan", [(i, i ^ bits) for i in range(n_chan)])

    def along(value, step):
        pairs = [(i, i + step) for i in range(n_section) if 0 <= i + step < n_section]
        return lax.ppermute(value, "section", pairs)

    wd = block_diagonal(conv_weight[0], pack)
    weights = point_weight[0]
    place = jnp.stack([(chip ^ k) * 2 + (parity ^ p) for k in range(chips) for p in range(2)]).astype(jnp.int32)
    other = split(place, weights, chips, 1)
    own = split(place, weights, chips, 0)
    twin = load(across(other, 1))
    turned = {}
    head_rows = jnp.pad(head_weight.T, ((0, CROWS - CLASSES), (0, 0)))

    order = sorted(range(1, chips), key=lambda k: -bin(k).count("1"))
    info = jnp.stack([section, jnp.int32(last)]).astype(jnp.int32)
    zero = [jnp.zeros((steps // CUTS, chans), BF16)] * CUTS
    kept, gone = [], []
    tops = {}
    heads, states = None, []

    def forward(r, recv):
        nonlocal kept
        cuts = AHEAD_CUTS if r < n_section - 1 else 1
        state, act, deriv = conv_forward(info, inputs[min(r, micro - 1)], recv, wd)
        act_twin = across(act, 1)
        arrived, sent, score = {}, [], []
        head = [heads] if r >= last else []
        for k in order:
            out = mix(act, act_twin, own, twin, k, cuts, *head, *score)
            score = list(out[cuts:])
            sent.append(out[0])
            arrived[k] = [across(cut, 2 * k) for cut in out[:cuts]]
        mine, *rest = mix_own(r, info, act, act_twin, own, twin, state, deriv, kept, micro, *head, *score)
        kept = rest[-3:]
        if r >= last:
            score = rest[0] + across(rest[0], 1)
            score = score + sum(across(score, 2 * k) for k in range(1, chips))
            tops[r - last] = top_back(score, labels[r - last][None, :], head_rows, LOSS_SCALE / (micro * steps))

        def finish(after):
            parts = [[arrived[k][i] for k in range(1, chips)] for i in range(cuts)]
            states.append([sum_state(mine, parts[i], i, cuts, after) for i in range(cuts)])
            return [along(state, 1) for state in states[-1]]

        return finish, sent + [mine]

    def backward(r, recv):
        nonlocal gone
        back = recv
        if r < micro:
            back = [choose(info, tops[r], recv[i], i) for i in range(CUTS)]
        pieces = {0: back}
        for k in order:
            pieces[k] = [None] * CUTS
        for i in range(CUTS):
            for k in order:
                pieces[k][i] = across(back[i], 2 * k)
        rest = list(range(1, chips))
        twins = {k: [across(cut, 1) for cut in pieces[k]] for k in range(chips)}
        onward = r + 1 < rounds
        terms = [(1, 0)] + [(0, k) for k in range(chips)]
        places = [1] + [2 * k for k in range(chips)]
        listed = twins[0] + [cut for k in range(chips) for cut in pieces[k]]
        acc, back_all = fold(r, info, listed, [turned["own"], turned["other"]], terms, places, micro, gone[:1])
        terms, places = [(0, k) for k in rest], [2 * k + 1 for k in rest]
        listed = [cut for k in rest for cut in twins[k]]
        *back, back_all, grad_all = conv_backward(
            r, info, acc, kept[2], turned["wd"], back, turned["other"], listed, terms, places, onward, back_all, gone[1:]
        )
        gone = [back_all, grad_all]
        return [along(cut, -1) for cut in back] if onward else None

    ahead, behind = zero, zero
    for t in range(rounds + n_section):
        if t < rounds:
            finish, made = forward(t, ahead)
        after = []
        if t == 0:
            own_turned, own_mark = turn(own, made[-1:])
            other_turned, other_mark = turn(other, made[-1:])
            wd_turned, wd_mark = turn(wd.reshape(-1, pack, pack), made[-1:])
            turned.update(own=own_turned, other=other_turned, wd=wd_turned.reshape(wd.shape))
            after = [own_mark, other_mark, wd_mark]
        if t == 1:
            after = [heads]
        if t >= n_section:
            behind = backward(t - n_section, behind)
        if t + 1 < rounds:
            ahead = finish(after)
        if t == 0:
            held = hold(head_rows, states[-1])
            heads = jnp.stack([held] + [across(held, 2 * k) for k in range(1, chips)])

    grad_point, grad_conv = grads(
        place, kept[0], gone[0], kept[1], gone[1], micro, point_weight.shape[2], taps, width, pack
    )
    return grad_point, grad_conv


def solution(mesh):
    placed = (
        P(None, None, "chan"),
        P(),
        P("section", None, None, "chan"),
        P("section", "chan", None),
        P("chan", None),
    )
    return jax.shard_map(
        local,
        mesh=mesh,
        in_specs=placed,
        out_specs=(P("section", "chan", None), P("section", None, None, "chan")),
        check_vma=False,
    )
```
